32 devices in a mesh: dp: 8 (over y, x, core), tensor: 4 (over z).
Axes of the slice: x: 2, y: 2, z: 4, core: 2. Of those that a mesh axis runs over, the one named last changes fastest.
Arguments:
- teacher_rows: bfloat16 [1024, 16384], P('dp', 'tensor'), may hold values from -6 to 6
- row_map: int32 [1024], P('dp'), may hold values from 0 to 1023, as said below
- student_hidden: bfloat16 [1024, 8192], P('dp', 'tensor'), may hold values from -6 to 6
- projected: bfloat16 [1024, 8192], P('dp', 'tensor'), may hold values from -6 to 6
- mlp_input: bfloat16 [1024, 8192], P('dp', 'tensor'), may hold values from -6 to 6
- gate_bucket: bfloat16 [8192, 512], P(None, 'tensor'), may hold values from -0.0625 to 0.0625
- up_bucket: bfloat16 [8192, 512], P(None, 'tensor'), may hold values from -0.0625 to 0.0625
- down_bucket: bfloat16 [512, 8192], P('tensor'), may hold values from -0.03125 to 0.03125
Outputs:
- grad_proj: float32 [128, 4, 4096], P(None, 'tensor', 'dp')
- grad_gate: float32 [512, 8192], P('tensor', 'dp')
- grad_up: float32 [512, 8192], P('tensor', 'dp')
The draws below stay inside these ranges and needn't reach their ends.
Inputs may be any that keep to these rules, and one draw needn't show every extreme that they name: `row_map`: a permutation of the token ids; token id t belongs to student group t // 128; the rows of one device (aligned blocks of 128) send exactly 16 rows to every student group.
All inputs are finite; a program needn't handle non-finite values.
Results may differ from the reference program's by a relative error of at most 0.0042.
Values may be sent and summed in bfloat16 or wider, within the bound.
No kernel may reach another device: no remote copies, remote signals or barrier semaphores. Data moves between devices by JAX's collectives and lax.ppermute only.
A program may use at most 128 MiB of HBM per device.

```python
import jax
import jax.numpy as jnp
from jax import lax

DS = 8192
DT = 16384
FF = 28672
TOK_DEV = 128
HB = 512
PB = 128
TOKENS = 1024
N_TENSOR = 4


def draw_row_map(key, part):
    key = jax.random.fold_in(key, 7)
    groups = TOKENS // TOK_DEV
    per_peer = TOK_DEV // groups
    first_key, second_key = jax.random.split(key)
    slot_perm = jax.vmap(lambda k: jax.random.permutation(k, TOK_DEV))(jax.random.split(first_key, groups))
    arranged = jax.vmap(lambda k: jax.random.permutation(k, TOK_DEV))(jax.random.split(second_key, groups))
    group_ids = arranged // per_peer
    offset = arranged % per_peer
    sources = jnp.arange(groups, dtype=jnp.int32)[:, None]
    slots = slot_perm[group_ids, sources * per_peer + offset]
    return (group_ids * TOK_DEV + slots).reshape(-1).astype(jnp.int32)


def with_spikes(array, stream_key, source, target, shards_of, factor):
    owner, partner = [(jnp.arange(array.shape[axis_at]) // (array.shape[axis_at] // shards_of)).reshape([-1 if axis == axis_at else 1 for axis in range(array.ndim)]) for axis_at in (source, target)]
    chosen = jax.random.permutation(stream_key, shards_of)[partner]
    strong = (owner == chosen) | (owner == (partner + shards_of // 2) % shards_of)
    return jnp.where(strong, factor * array, array)


def block_scale(key, extent, cuts, low, top_value):
    loudness, own = 1.0, jax.random.fold_in(key, 6)
    for axis_at, parts in cuts:
        heights = jnp.exp(jax.random.uniform(jax.random.fold_in(own, axis_at), (parts,), jnp.float32, low / len(cuts), top_value / len(cuts)))
        loudness = loudness * jnp.repeat(heights, extent[axis_at] // parts).reshape([-1 if axis == axis_at else 1 for axis in range(len(extent))])
    return loudness


def bell_draw(stream_key, shape, width, bound, cuts=(), kind=jnp.bfloat16):
    result = jax.random.normal(stream_key, shape, jnp.float32) * width
    if len(cuts) > 0:
        result = block_scale(stream_key, shape, cuts, -0.22, 0.18) * result
    return jnp.clip(result, min=-bound, max=bound).astype(kind)


def noise_with(rng, extent, width, most, shards, heavy, kind=jnp.bfloat16):
    entries = width * jax.random.normal(rng, extent, jnp.float32)
    if shards:
        entries = entries * block_scale(rng, extent, shards, -0.22, 0.18)
    return jnp.clip(with_spikes(entries, jax.random.fold_in(rng, 3), *heavy), -most, most).astype(kind)


def setup_inputs(seed: int = 0) -> dict:
    key_list = jax.random.split(jax.random.key(seed), 9)
    return {
        "teacher_rows": noise_with(key_list[0], (TOKENS, DT), 1.0, 6.0, ((0, 8), (1, 4)), (0, 1, 8, 2.0)),
        "row_map": draw_row_map(jax.random.fold_in(key_list[8], 71), 0),
        "student_hidden": bell_draw(key_list[2], (TOKENS, DS), 1.0, 6.0, ((0, 8), (1, 4))),
        "projected": bell_draw(key_list[3], (TOKENS, DS), 1.0, 6.0, ((0, 8), (1, 4))),
        "mlp_input": noise_with(key_list[4], (TOKENS, DS), 1.0, 6.0, ((0, 8), (1, 4)), (0, 1, 8, 2.0)),
        "gate_bucket": bell_draw(key_list[5], (DS, HB), DS ** -0.5, 0.0625, ((1, 4),)),
        "up_bucket": bell_draw(key_list[6], (DS, HB), DS ** -0.5, 0.0625, ((1, 4),)),
        "down_bucket": bell_draw(key_list[7], (HB, DS), FF ** -0.5, 0.03125, ((0, 4),)),
    }


def reference(teacher_rows, row_map, student_hidden, projected, mlp_input, gate_bucket, up_bucket, down_bucket):
    handed = jnp.zeros((TOKENS, DT), jnp.bfloat16).at[row_map].set(teacher_rows)
    factor = float(TOKENS) ** -0.5
    err = ((student_hidden.astype(jnp.float32) - projected.astype(jnp.float32)) * factor).astype(jnp.bfloat16)
    proj_full = lax.dot_general(err[:, :PB], handed, (((0,), (0,)), ((), ())), preferred_element_type=jnp.float32)
    grad_proj = proj_full.reshape(PB, N_TENSOR, DT // N_TENSOR)
    act_grad = lax.dot_general(err, down_bucket, (((1,), (1,)), ((), ())), preferred_element_type=jnp.float32)
    gate_pre = jnp.dot(mlp_input, gate_bucket, preferred_element_type=jnp.float32)
    up_pre = jnp.dot(mlp_input, up_bucket, preferred_element_type=jnp.float32)
    sigmoid_gate = jax.nn.sigmoid(gate_pre)
    gate_grad = (act_grad * up_pre * sigmoid_gate * (1.0 + gate_pre * (1.0 - sigmoid_gate))).astype(jnp.bfloat16)
    up_grad = (act_grad * gate_pre * sigmoid_gate).astype(jnp.bfloat16)
    grad_gate = lax.dot_general(gate_grad, mlp_input, (((0,), (0,)), ((), ())), preferred_element_type=jnp.float32)
    grad_up = lax.dot_general(up_grad, mlp_input, (((0,), (0,)), ((), ())), preferred_element_type=jnp.float32)
    return (grad_proj, grad_gate, grad_up)
```

```python
import math

import jax
import jax.numpy as jnp
from jax import lax
from jax.experimental import pallas as pl
from jax.experimental.pallas import tpu as pltpu
from jax.sharding import PartitionSpec as P

PB = 128
LANES = 128
GROUP = 8
FIRST = 96
MIB = 1 << 20

VMEM = pl.BlockSpec(memory_space=pltpu.VMEM)


def params(mib):
    return pltpu.CompilerParams(vmem_limit_bytes=mib * MIB)


def cost(flops, nbytes):
    return pl.CostEstimate(flops=int(flops), bytes_accessed=int(nbytes), transcendentals=0)


def struct(shape, dtype=jnp.bfloat16):
    return jax.ShapeDtypeStruct(shape, dtype)


def shift(x, count, by):
    return lax.ppermute(x, "tensor", [(i, (i + by) % count) for i in range(count)])


def swap(x, count, mask):
    return lax.ppermute(x, "dp", [(i, i ^ mask) for i in range(count)])


def contract_rows(left, right):
    return lax.dot_general(
        left, right, (((0,), (0,)), ((), ())), preferred_element_type=jnp.float32
    )


def contract_cols(left, right):
    return lax.dot_general(
        left, right, (((1,), (1,)), ((), ())), preferred_element_type=jnp.float32
    )


def scaled_difference(student, projected, factor):
    wide = student.astype(jnp.float32) - projected.astype(jnp.float32)
    return (wide * factor).astype(jnp.bfloat16)


def prepare(row_map, teacher, mlp_input, student, projected, down, n_dp, n_t, rows, factor):
    tok, width = mlp_input.shape
    wide = teacher.shape[1] // n_dp
    second = tok - FIRST
    hbm = pl.BlockSpec(memory_space=pltpu.HBM)
    if wide % LANES:
        blocks = teacher.reshape(tok, n_dp, wide).transpose(1, 0, 2)
        wide = 0

    def kernel(m_ref, t_ref, x_ref, s_ref, p_ref, d_ref, one_ref, two_ref, *refs):
        pieces, outs, (s_buf, p_buf, m_buf, sems) = refs[:n_t], refs[n_t:-4], refs[-4:]
        row = pl.multiple_of((lax.axis_index("dp") % GROUP) * rows, rows)
        pairs = [
            (s_ref.at[:, :PB], s_buf),
            (p_ref.at[:, :PB], p_buf),
            (m_ref, m_buf),
            (x_ref.at[:FIRST], one_ref.at[:, :width]),
            (x_ref.at[FIRST:], two_ref),
        ]
        for k in range(n_t):
            col = pl.multiple_of(((lax.axis_index("tensor") + k) % n_t) * width, width)
            pairs.append((d_ref.at[pl.ds(row, rows), pl.ds(col, width)], pieces[k]))
        if wide:
            for i in range(n_dp):
                pairs.append((t_ref.at[:, i * wide : (i + 1) * wide], outs[0].at[i]))
        copies = [
            pltpu.make_async_copy(src, dst, sems.at[i]) for i, (src, dst) in enumerate(pairs)
        ]
        for c in copies:
            c.start()
        for c in copies[:3]:
            c.wait()
        bucket = scaled_difference(s_buf[...], p_buf[...], factor)
        one_ref[:, width : width + PB] = bucket[:FIRST]
        one_ref[:second, width + PB :] = bucket[FIRST:]
        one_ref[second + 16 :, width + PB :] = jnp.zeros((FIRST - second - 16, PB), jnp.bfloat16)
        line = lax.broadcasted_iota(jnp.int32, (16, tok), 0)
        number = jnp.broadcast_to(m_buf[...], (16, tok))
        high, low = number // LANES, number % LANES
        digits = jnp.where(line == 0, high, jnp.where(line == 1, low, 0))
        one_ref[second : second + 16, width + PB :] = digits.astype(jnp.float32).astype(jnp.bfloat16)
        for c in copies[3:]:
            c.wait()

    shapes = [(FIRST, width + 2 * PB), (second, width)] + [(rows, width)] * n_t
    if wide:
        shapes.append((n_dp, tok, wide))
    count = 5 + n_t + n_dp
    out = pl.pallas_call(
        kernel,
        in_specs=[hbm] * 6,
        out_specs=[VMEM] * len(shapes),
        out_shape=[struct(s) for s in shapes],
        scratch_shapes=[
            pltpu.VMEM((tok, PB), jnp.bfloat16),
            pltpu.VMEM((tok, PB), jnp.bfloat16),
            pltpu.VMEM((1, tok), jnp.int32),
            pltpu.SemaphoreType.DMA((count,)),
        ],
        compiler_params=params(60),
        cost_estimate=cost(0, 1024),
        name="prepare",
    )(row_map.reshape(1, tok), teacher, mlp_input, student, projected, down)
    return out if wide else [*out, blocks]


def stack_rows(parts, after=()):
    height = [p.shape[0] for p in parts]

    def kernel(*refs):
        out_ref, at = refs[-1], 0
        for ref, h in zip(refs, height):
            out_ref[at : at + h] = ref[...]
            at += h

    return pl.pallas_call(
        kernel,
        in_specs=[VMEM] * len(parts) + [pl.BlockSpec(memory_space=pl.ANY)] * len(after),
        out_specs=VMEM,
        out_shape=struct((sum(height),) + parts[0].shape[1:]),
        compiler_params=params(16),
        cost_estimate=cost(0, 1024),
        name="stack_rows",
    )(*parts, *after)


def join(gate, up, student, projected, factor, after):
    def kernel(gate_ref, up_ref, s_ref, p_ref, *refs):
        w_ref, err_ref = refs[len(after) :]
        hb = gate_ref.shape[1]
        w_ref[:, :hb] = gate_ref[...]
        w_ref[:, hb:] = up_ref[...]
        err_ref[...] = scaled_difference(s_ref[...], p_ref[...], factor)

    return pl.pallas_call(
        kernel,
        in_specs=[VMEM] * 4 + [pl.BlockSpec(memory_space=pl.ANY)] * len(after),
        out_specs=[VMEM] * 2,
        out_shape=[struct((gate.shape[0], 2 * gate.shape[1])), struct(student.shape)],
        compiler_params=params(24),
        cost_estimate=cost(0, 1024),
        name="join",
    )(gate, up, student, projected, *after)


def ordered(x, *after):
    def kernel(*refs):
        pass

    return pl.pallas_call(
        kernel,
        in_specs=[pl.BlockSpec(memory_space=pl.ANY)] * (1 + len(after)),
        out_specs=pl.BlockSpec(memory_space=pl.ANY),
        out_shape=struct(x.shape, x.dtype),
        input_output_aliases={0: 0},
        cost_estimate=cost(0, 1024),
        name="ordered",
    )(x, *after)


def partial_products(near, far, err, n_t, rows, after):
    tok, width = err.shape
    hb = rows * GROUP
    half = GROUP // 2

    def kernel(near_ref, far_ref, e_ref, *refs):
        outs = refs[len(after) :]
        place = lax.axis_index("dp") % GROUP
        for side, ref in enumerate((near_ref, far_ref)):
            product = contract_cols(ref[...], e_ref[...])
            for j in range(half):
                row = pl.multiple_of((place ^ (2 * j + side)) * rows, rows)
                for k in range(n_t):
                    at = (j * n_t + k) * rows
                    outs[k][pl.ds(row, rows), :] = product[at : at + rows]

    return pl.pallas_call(
        kernel,
        in_specs=[VMEM] * 3
        + [pl.BlockSpec(memory_space=pl.ANY)] * len(after),
        out_specs=[VMEM] * n_t,
        out_shape=[struct((hb, tok), jnp.float32)] * n_t,
        compiler_params=params(16),
        cost_estimate=cost(0, 1024),
        name="partial_products",
    )(near, far, err, *after)


def features(slices, weights, n_dp, rest=None, after=()):
    n_t = len(slices)
    count, width = slices[0].shape[0], weights.shape[0] // n_t
    hb = weights.shape[1] // 2
    cols = width * n_t // n_dp
    per = width // cols
    if rest is None:
        base = 2 * PB
        others = []
    else:
        pre, acts = rest
        tok = pre.shape[0] + count
        base = (tok // count) * 2 * hb
        others = [pre, *acts]

    def kernel(*refs):
        xs, refs = refs[:n_t], refs[n_t:]
        w_ref, refs = refs[0], refs[1:]
        if rest is None:
            out_ref, pre_ref, bucket_ref = refs[len(after) :]
        else:
            pre_ref, act_refs, out_ref = refs[0], refs[1 : 1 + n_t], refs[-1]
        pre = jnp.zeros((count, 2 * hb), jnp.float32)
        for k in range(n_t):
            slot = (lax.axis_index("tensor") + n_t - k) % n_t
            at = pl.ds(pl.multiple_of(slot * width, width), width)
            x = xs[k][:, :width]
            pre += jnp.dot(x, w_ref[at, :], preferred_element_type=jnp.float32)
            for b in range(per):
                out_ref[slot * per + b, :, base:] = xs[k][:, b * cols : (b + 1) * cols]
            if rest is None:

                @pl.when(slot == 0)
                def _(k=k):
                    bucket_ref[...] = xs[k][:, width:]

        if rest is None:
            pre_ref[...] = pre
            for i in range(n_dp):
                out_ref[i, :, :base] = bucket_ref[...]
            return
        act = act_refs[0][...]
        for ref in act_refs[1:]:
            act += ref[...]
        act = act.T
        pre = jnp.concatenate([pre_ref[...], pre])
        gate_pre, up_pre = pre[:, :hb], pre[:, hb:]
        s = jax.nn.sigmoid(gate_pre)
        gate_grad = (act * up_pre * s * (1.0 + gate_pre * (1.0 - s))).astype(jnp.bfloat16)
        up_grad = (act * gate_pre * s).astype(jnp.bfloat16)
        for b in range(tok // count):
            for j, grad in enumerate((gate_grad, up_grad)):
                part = grad[b * count : (b + 1) * count]
                for i in range(n_dp):
                    out_ref[i, :, (2 * b + j) * hb : (2 * b + j + 1) * hb] = part

    payload = struct((n_dp, count, base + cols))
    first = rest is None
    return pl.pallas_call(
        kernel,
        in_specs=[VMEM] * (n_t + 1 + len(others)) + [pl.BlockSpec(memory_space=pl.ANY)] * len(after),
        out_specs=[VMEM, VMEM] if first else VMEM,
        out_shape=[payload, struct((count, 2 * hb), jnp.float32)] if first else payload,
        scratch_shapes=[pltpu.VMEM((count, 2 * PB), jnp.bfloat16)] if first else [],
        compiler_params=params(24),
        cost_estimate=cost(0, 1024),
        name="first_features" if first else "last_features",
    )(*slices, weights, *others, *after)


def projector(came, teach):
    n_dp, tok, wide = teach.shape
    second = tok - FIRST
    groups = n_dp // GROUP
    span = GROUP * tok

    def kernel(came_ref, teach_ref, out_ref, flipped_ref):
        def flip(g, carry):
            parts = []
            for i in range(GROUP):
                parts.append(came_ref[g * GROUP + i, :, :PB])
                parts.append(came_ref[g * GROUP + i, :second, PB : 2 * PB])
            flipped_ref[g] = jnp.concatenate(parts).astype(jnp.float32).T.astype(jnp.bfloat16)
            return carry

        lax.fori_loop(0, groups, flip, 0)
        out_ref[...] = jnp.zeros_like(out_ref)

        def sender(g, carry):
            digits = came_ref[g, second : second + 16, PB : 2 * PB].astype(jnp.float32)
            number = (digits[0:1] * float(LANES) + digits[1:2]).astype(jnp.int32)

            def block(h, total):
                token = lax.broadcasted_iota(jnp.int32, (span, tok), 0) + h * span
                picks = (token == number).astype(jnp.float32).astype(jnp.bfloat16)
                return total + jnp.dot(flipped_ref[h], picks, preferred_element_type=jnp.float32)

            rows = lax.fori_loop(0, groups, block, jnp.zeros((PB, tok), jnp.float32))
            out_ref[...] += jnp.dot(
                rows.astype(jnp.bfloat16), teach_ref[g], preferred_element_type=jnp.float32
            )
            return carry

        lax.fori_loop(0, n_dp, sender, 0)

    return pl.pallas_call(
        kernel,
        in_specs=[VMEM, VMEM],
        out_specs=VMEM,
        out_shape=struct((PB, wide), jnp.float32),
        scratch_shapes=[pltpu.VMEM((groups, PB, span), jnp.bfloat16)],
        compiler_params=params(24),
        cost_estimate=cost(0, 1024),
        name="projector",
    )(came, teach)


def final_product(first, last, hb, cols):
    n_dp, count = last.shape[:2]
    blocks = (last.shape[2] - cols) // (2 * hb)

    def kernel(first_ref, last_ref, gate_ref, up_ref):
        def group(g, total):
            here = pl.ds(g * GROUP, GROUP)
            for b in range(blocks):
                grads = last_ref[here, :, 2 * b * hb : 2 * (b + 1) * hb]
                if b < blocks - 1:
                    feats = first_ref[here, b * count : (b + 1) * count, 2 * PB :]
                else:
                    feats = last_ref[here, :, 2 * blocks * hb :]
                total = total + contract_rows(
                    grads.reshape(GROUP * count, 2 * hb), feats.reshape(GROUP * count, cols)
                )
            return total

        total = jnp.zeros((2 * hb, cols), jnp.float32)
        if n_dp == GROUP:
            total = group(0, total)
        else:
            total = lax.fori_loop(0, n_dp // GROUP, group, total)
        gate_ref[...] = total[:hb]
        up_ref[...] = total[hb:]

    return pl.pallas_call(
        kernel,
        in_specs=[VMEM] * 2,
        out_specs=[VMEM] * 2,
        out_shape=[struct((hb, cols), jnp.float32)] * 2,
        compiler_params=params(24),
        cost_estimate=cost(0, 1024),
        name="final_product",
    )(first, last)


def body(
    teacher_rows, row_map, student_hidden, projected, mlp_input, gate_bucket, up_bucket, down_bucket
):
    tok = row_map.shape[0]
    n_dp = lax.axis_size("dp")
    n_t = lax.axis_size("tensor")
    hb, width = down_bucket.shape[0], student_hidden.shape[1]
    cols = width * n_t // n_dp
    factor = 1.0 / math.sqrt(tok * n_dp)
    rows = hb // GROUP

    one, two, *pieces, teach = prepare(
        row_map, teacher_rows, mlp_input, student_hidden, projected, down_bucket,
        n_dp, n_t, rows, factor,
    )
    teach = lax.all_to_all(teach, "dp", split_axis=0, concat_axis=0, tiled=True)

    pieces = [pieces[0]] + [shift(pieces[k], n_t, k) for k in range(1, n_t)]
    before, beyond = shift(one, n_t, 1), shift(one, n_t, -1)
    mine = stack_rows(pieces)
    weights, err = join(gate_bucket, up_bucket, student_hidden, projected, factor, after=[mine])
    before = ordered(before, mine, weights)
    first = [one, before, shift(before, n_t, 1), beyond]
    others = [swap(mine, n_dp, mask) for mask in (2, 4, 6)]
    near = stack_rows([mine] + others)
    far = swap(near, n_dp, 1)
    before, beyond = shift(two, n_t, 1), shift(two, n_t, -1)
    second = [two, before, shift(before, n_t, 1), beyond]

    sent, pre = features(first, weights, n_dp, after=[near])
    came_first = lax.all_to_all(sent, "dp", split_axis=0, concat_axis=0, tiled=True)

    partial = partial_products(near, far, err, n_t, rows, after=[pre, before, beyond, teach])
    acts = [partial[0]] + [shift(partial[k], n_t, -k) for k in range(1, n_t)]

    sent = features(second, weights, n_dp, rest=(pre, acts))
    came_last = lax.all_to_all(sent, "dp", split_axis=0, concat_axis=0, tiled=True)
    grad_proj = projector(came_first, teach)
    grad_gate, grad_up = final_product(came_first, came_last, hb, cols)
    return (grad_proj[:, None, :], grad_gate, grad_up)


def solution(mesh):
    in_specs = (
        P("dp", "tensor"),
        P("dp"),
        P("dp", "tensor"),
        P("dp", "tensor"),
        P("dp", "tensor"),
        P(None, "tensor"),
        P(None, "tensor"),
        P("tensor", None),
    )
    out_specs = (P(None, "tensor", "dp"), P("tensor", "dp"), P("tensor", "dp"))
    return jax.shard_map(body, mesh=mesh, in_specs=in_specs, out_specs=out_specs, check_vma=False)
```

```python
import math

import jax
import jax.numpy as jnp
from jax import lax
from jax.experimental import pallas as pl
from jax.experimental.pallas import tpu as pltpu
from jax.sharding import PartitionSpec as P

PB = 128
LANES = 128
GROUP = 8
FIRST = 80
MIB = 1 << 20

VMEM = pl.BlockSpec(memory_space=pltpu.VMEM)


def params(mib):
    return pltpu.CompilerParams(vmem_limit_bytes=mib * MIB)


def cost(flops, nbytes):
    return pl.CostEstimate(flops=int(flops), bytes_accessed=int(nbytes), transcendentals=0)


def struct(shape, dtype=jnp.bfloat16):
    return jax.ShapeDtypeStruct(shape, dtype)


def shift(x, count, by):
    return lax.ppermute(x, "tensor", [(i, (i + by) % count) for i in range(count)])


def swap(x, count, mask):
    return lax.ppermute(x, "dp", [(i, i ^ mask) for i in range(count)])


def contract_rows(left, right):
    return lax.dot_general(
        left, right, (((0,), (0,)), ((), ())), preferred_element_type=jnp.float32
    )


def contract_cols(left, right):
    return lax.dot_general(
        left, right, (((1,), (1,)), ((), ())), preferred_element_type=jnp.float32
    )


def scaled_difference(student, projected, factor):
    wide = student.astype(jnp.float32) - projected.astype(jnp.float32)
    return (wide * factor).astype(jnp.bfloat16)


def prepare(row_map, teacher, mlp_input, student, projected, down, n_dp, n_t, factor):
    tok, width = mlp_input.shape
    rows = down.shape[0] // GROUP
    wide = teacher.shape[1] // n_dp
    second = tok - FIRST
    hbm = pl.BlockSpec(memory_space=pltpu.HBM)
    if wide % LANES:
        blocks = teacher.reshape(tok, n_dp, wide).transpose(1, 0, 2)
        wide = 0

    def kernel(m_ref, t_ref, x_ref, s_ref, p_ref, d_ref, right_ref, left_ref, *refs):
        two_ref, digits_ref, here_ref, far_ref = refs[:4]
        s_buf, p_buf, m_buf, sems = refs[-4:]
        row = pl.multiple_of((lax.axis_index("dp") % GROUP) * rows, rows)
        pairs = [
            (s_ref.at[:, :PB], s_buf),
            (p_ref.at[:, :PB], p_buf),
            (m_ref, m_buf),
            (x_ref.at[:FIRST], right_ref.at[:FIRST, :width]),
            (x_ref.at[:FIRST], left_ref.at[:FIRST, :width]),
            (x_ref.at[FIRST:], two_ref),
        ]
        pieces = [here_ref, right_ref.at[FIRST:, :width], far_ref, left_ref.at[FIRST:, :width]]
        for k in range(n_t):
            col = pl.multiple_of(((lax.axis_index("tensor") + k) % n_t) * width, width)
            pairs.append((d_ref.at[pl.ds(row, rows), pl.ds(col, width)], pieces[k]))
        if wide:
            for i in range(n_dp):
                pairs.append((t_ref.at[:, i * wide : (i + 1) * wide], refs[4].at[i]))
        copies = [
            pltpu.make_async_copy(src, dst, sems.at[i]) for i, (src, dst) in enumerate(pairs)
        ]
        for c in copies:
            c.start()
        for c in copies[:3]:
            c.wait()
        bucket = scaled_difference(s_buf[...], p_buf[...], factor)
        for ref in (right_ref, left_ref):
            ref[:FIRST, width : width + PB] = bucket[:FIRST]
            ref[:second, width + PB :] = bucket[FIRST:]
            ref[second:, width + PB :] = jnp.zeros((FIRST + rows - second, PB), jnp.bfloat16)
            ref[FIRST:, width : width + PB] = jnp.zeros((rows, PB), jnp.bfloat16)
        line = lax.broadcasted_iota(jnp.int32, (16, tok), 0)
        number = jnp.broadcast_to(m_buf[...], (16, tok))
        high, low = number // LANES, number % LANES
        digits = jnp.where(line == 0, high, jnp.where(line == 1, low, 0))
        digits_ref[...] = digits.astype(jnp.float32).astype(jnp.bfloat16)
        for c in copies[3:]:
            c.wait()

    shapes = [(FIRST + rows, width + 2 * PB)] * 2 + [(second, width), (16, tok)] + [(rows, width)] * 2
    if wide:
        shapes.append((n_dp, tok, wide))
    out = pl.pallas_call(
        kernel,
        in_specs=[hbm] * 6,
        out_specs=[VMEM] * len(shapes),
        out_shape=[struct(s) for s in shapes],
        scratch_shapes=[
            pltpu.VMEM((tok, PB), jnp.bfloat16),
            pltpu.VMEM((tok, PB), jnp.bfloat16),
            pltpu.VMEM((1, tok), jnp.int32),
            pltpu.SemaphoreType.DMA((6 + n_t + n_dp,)),
        ],
        compiler_params=params(60),
        cost_estimate=cost(0, 1024),
        name="prepare",
    )(row_map.reshape(1, tok), teacher, mlp_input, student, projected, down)
    return out if wide else [*out, blocks]


def stack_rows(parts, rows, width, after=()):
    def kernel(*refs):
        out_ref = refs[-1]
        for i, ref in enumerate(refs[: len(parts)]):
            out_ref[i * rows : (i + 1) * rows] = ref[ref.shape[0] - rows :, :width]

    return pl.pallas_call(
        kernel,
        in_specs=[VMEM] * len(parts) + [pl.BlockSpec(memory_space=pl.ANY)] * len(after),
        out_specs=VMEM,
        out_shape=struct((len(parts) * rows, width)),
        compiler_params=params(8),
        cost_estimate=cost(0, 1024),
        name="stack_rows",
    )(*parts, *after)


def partial_products(near, far, student, projected, n_t, rows, factor, after):
    tok, width = student.shape
    hb = rows * GROUP
    half = GROUP // 2

    def kernel(near_ref, far_ref, s_ref, p_ref, *refs):
        outs = refs[len(after) :]
        err = scaled_difference(s_ref[...], p_ref[...], factor)
        place = lax.axis_index("dp") % GROUP
        for side, ref in enumerate((near_ref, far_ref)):
            product = contract_cols(ref[...], err)
            for j in range(half):
                row = pl.multiple_of((place ^ (2 * j + side)) * rows, rows)
                for k in range(n_t):
                    at = (j * n_t + k) * rows
                    outs[k][pl.ds(row, rows), :] = product[at : at + rows]

    return pl.pallas_call(
        kernel,
        in_specs=[VMEM] * 4
        + [pl.BlockSpec(memory_space=pl.ANY)] * len(after),
        out_specs=[VMEM] * n_t,
        out_shape=[struct((hb, tok), jnp.float32)] * n_t,
        compiler_params=params(60),
        cost_estimate=cost(0, 1024),
        name="partial_products",
    )(near, far, student, projected, *after)


def features(slices, gate, up, n_dp, digits=None, rest=None, after=()):
    n_t = len(slices)
    width, hb = gate.shape[0] // n_t, gate.shape[1]
    cols = width * n_t // n_dp
    per = width // cols
    first = rest is None
    if first:
        count, base, others = FIRST, 2 * PB, [digits]
        second = digits.shape[1] - FIRST
    else:
        count, others = slices[0].shape[0], [rest[0], *rest[1]]
        base = (1 + pl.cdiv(FIRST, count)) * 2 * hb

    def kernel(*refs):
        xs, gate_ref, up_ref, refs = refs[:n_t], refs[n_t], refs[n_t + 1], refs[n_t + 2 :]
        w_ref, sems = refs[-2:]
        if first:
            digits_ref, (out_ref, pre_ref) = refs[0], refs[-4:-2]
        else:
            pre_ref, act_refs, out_ref = refs[0], refs[1 : 1 + n_t], refs[-3]
        t = lax.axis_index("tensor")
        slots = [(t + n_t - k) % n_t for k in range(n_t)]
        copies = []
        for k in range(n_t):
            at = pl.ds(pl.multiple_of(slots[k] * width, width), width)
            for j, ref in enumerate((gate_ref, up_ref)):
                copies.append(
                    pltpu.make_async_copy(
                        ref.at[at], w_ref.at[k, :, j * hb : (j + 1) * hb], sems.at[2 * k + j]
                    )
                )
        for c in copies:
            c.start()
        for k in range(n_t):
            for b in range(per):
                out_ref[slots[k] * per + b, :, base:] = xs[k][:count, b * cols : (b + 1) * cols]
            if first:

                @pl.when(slots[k] == 0)
                def _(k=k):
                    for i in range(n_dp):
                        out_ref[i, :, :base] = xs[k][:count, width:]

        if first:
            for i in range(n_dp):
                out_ref[i, second : second + 16, PB : 2 * PB] = digits_ref[...]
        pre = jnp.zeros((count, 2 * hb), jnp.float32)
        for k in range(n_t):
            copies[2 * k].wait()
            copies[2 * k + 1].wait()
            pre += jnp.dot(xs[k][:count, :width], w_ref[k], preferred_element_type=jnp.float32)
        if first:
            pre_ref[...] = pre
            return
        act = act_refs[0][...]
        for ref in act_refs[1:]:
            act += ref[...]
        act = act.T
        pre = jnp.concatenate([pre_ref[...], pre])
        gate_pre, up_pre = pre[:, :hb], pre[:, hb:]
        s = jax.nn.sigmoid(gate_pre)
        gate_grad = (act * up_pre * s * (1.0 + gate_pre * (1.0 - s))).astype(jnp.bfloat16)
        up_grad = (act * gate_pre * s).astype(jnp.bfloat16)
        starts = [*range(0, FIRST, count), FIRST]
        for b, low in enumerate(starts):
            size = min(count, FIRST - low) if low < FIRST else count
            for j, grad in enumerate((gate_grad, up_grad)):
                at = slice((2 * b + j) * hb, (2 * b + j + 1) * hb)
                for i in range(n_dp):
                    out_ref[i, :size, at] = grad[low : low + size]
                    if size < count:
                        out_ref[i, size:, at] = jnp.zeros((count - size, hb), jnp.bfloat16)

    payload = struct((n_dp, count, base + cols))
    anywhere = pl.BlockSpec(memory_space=pl.ANY)
    return pl.pallas_call(
        kernel,
        in_specs=[VMEM] * n_t
        + [pl.BlockSpec(memory_space=pltpu.HBM)] * 2
        + [VMEM] * len(others)
        + [anywhere] * len(after),
        out_specs=[VMEM, VMEM] if first else VMEM,
        out_shape=[payload, struct((count, 2 * hb), jnp.float32)] if first else payload,
        scratch_shapes=[
            pltpu.VMEM((n_t, width, 2 * hb), jnp.bfloat16),
            pltpu.SemaphoreType.DMA((2 * n_t,)),
        ],
        compiler_params=params(60),
        cost_estimate=cost(0, 1024),
        name="first_features" if first else "last_features",
    )(*slices, gate, up, *others, *after)


def projector(came, teach):
    n_dp, tok, wide = teach.shape
    second = tok - FIRST
    groups = n_dp // GROUP
    span = GROUP * tok

    def kernel(came_ref, teach_ref, out_ref, flipped_ref):
        def flip(g, carry):
            parts = []
            for i in range(GROUP):
                parts.append(came_ref[g * GROUP + i, :, :PB])
                parts.append(came_ref[g * GROUP + i, :second, PB : 2 * PB])
            flipped_ref[g] = jnp.concatenate(parts).astype(jnp.float32).T.astype(jnp.bfloat16)
            return carry

        lax.fori_loop(0, groups, flip, 0)
        out_ref[...] = jnp.zeros_like(out_ref)

        def sender(g, carry):
            digits = came_ref[g, second : second + 16, PB : 2 * PB].astype(jnp.float32)
            number = (digits[0:1] * float(LANES) + digits[1:2]).astype(jnp.int32)

            def block(h, total):
                token = lax.broadcasted_iota(jnp.int32, (span, tok), 0) + h * span
                picks = (token == number).astype(jnp.float32).astype(jnp.bfloat16)
                return total + jnp.dot(flipped_ref[h], picks, preferred_element_type=jnp.float32)

            rows = lax.fori_loop(0, groups, block, jnp.zeros((PB, tok), jnp.float32))
            out_ref[...] += jnp.dot(
                rows.astype(jnp.bfloat16), teach_ref[g], preferred_element_type=jnp.float32
            )
            return carry

        lax.fori_loop(0, n_dp, sender, 0)

    return pl.pallas_call(
        kernel,
        in_specs=[VMEM, VMEM],
        out_specs=VMEM,
        out_shape=struct((PB, wide), jnp.float32),
        scratch_shapes=[pltpu.VMEM((groups, PB, span), jnp.bfloat16)],
        compiler_params=params(24),
        cost_estimate=cost(0, 1024),
        name="projector",
    )(came, teach)


def final_product(first, last, hb, cols):
    n_dp, count = last.shape[:2]
    blocks = (last.shape[2] - cols) // (2 * hb)

    def kernel(first_ref, last_ref, gate_ref, up_ref):
        def group(g, total):
            here = pl.ds(g * GROUP, GROUP)
            for b in range(blocks):
                size = count
                if b < blocks - 1:
                    size = min(count, FIRST - b * count)
                    feats = first_ref[here, b * count : b * count + size, 2 * PB :]
                else:
                    feats = last_ref[here, :, 2 * blocks * hb :]
                grads = last_ref[here, :size, 2 * b * hb : 2 * (b + 1) * hb]
                total = total + contract_rows(
                    grads.reshape(GROUP * size, 2 * hb), feats.reshape(GROUP * size, cols)
                )
            return total

        total = jnp.zeros((2 * hb, cols), jnp.float32)
        if n_dp == GROUP:
            total = group(0, total)
        else:
            total = lax.fori_loop(0, n_dp // GROUP, group, total)
        gate_ref[...] = total[:hb]
        up_ref[...] = total[hb:]

    return pl.pallas_call(
        kernel,
        in_specs=[VMEM] * 2,
        out_specs=[VMEM] * 2,
        out_shape=[struct((hb, cols), jnp.float32)] * 2,
        compiler_params=params(24),
        cost_estimate=cost(0, 1024),
        name="final_product",
    )(first, last)


def body(
    teacher_rows, row_map, student_hidden, projected, mlp_input, gate_bucket, up_bucket, down_bucket
):
    tok = row_map.shape[0]
    n_dp = lax.axis_size("dp")
    n_t = lax.axis_size("tensor")
    hb, width = down_bucket.shape[0], student_hidden.shape[1]
    cols = width * n_t // n_dp
    factor = 1.0 / math.sqrt(tok * n_dp)
    rows = hb // GROUP

    right, left, two, digits, here, away, teach = prepare(
        row_map, teacher_rows, mlp_input, student_hidden, projected, down_bucket, n_dp, n_t, factor
    )
    before, beyond = shift(right, n_t, 1), shift(left, n_t, -1)
    away = shift(away, n_t, 2)
    teach = lax.all_to_all(teach, "dp", split_axis=0, concat_axis=0, tiled=True)

    mine = stack_rows([here, before, away, beyond], rows, width)
    one = shift(before, n_t, 1)
    others = [swap(mine, n_dp, mask) for mask in (2, 4, 6)]
    near = stack_rows([mine] + others, n_t * rows, width, after=[teach, one])
    far = swap(near, n_dp, 1)

    sent, pre = features(
        [right, before, one, beyond], gate_bucket, up_bucket, n_dp, digits, after=[near]
    )
    came_first = lax.all_to_all(sent, "dp", split_axis=0, concat_axis=0, tiled=True)

    before, beyond = shift(two, n_t, 1), shift(two, n_t, -1)
    one = shift(before, n_t, 1)
    partial = partial_products(
        near, far, student_hidden, projected, n_t, rows, factor, after=[pre, before, beyond]
    )
    acts = [partial[0]] + [shift(partial[k], n_t, -k) for k in range(1, n_t)]

    sent = features([two, before, one, beyond], gate_bucket, up_bucket, n_dp, rest=(pre, acts))
    came_last = lax.all_to_all(sent, "dp", split_axis=0, concat_axis=0, tiled=True)
    grad_proj = projector(came_first, teach)
    grad_gate, grad_up = final_product(came_first, came_last, hb, cols)
    return (grad_proj[:, None, :], grad_gate, grad_up)


def solution(mesh):
    in_specs = (
        P("dp", "tensor"),
        P("dp"),
        P("dp", "tensor"),
        P("dp", "tensor"),
        P("dp", "tensor"),
        P(None, "tensor"),
        P(None, "tensor"),
        P("tensor", None),
    )
    out_specs = (P(None, "tensor", "dp"), P("tensor", "dp"), P("tensor", "dp"))
    return jax.shard_map(body, mesh=mesh, in_specs=in_specs, out_specs=out_specs, check_vma=False)
```

```python
import functools
import math

import jax
import jax.numpy as jnp
from jax import lax
from jax.experimental import pallas as pl
from jax.experimental.pallas import tpu as pltpu
from jax.sharding import PartitionSpec as P

PB = 128
LANES = 128
GROUP = 8
MIB = 1 << 20

VMEM = pl.BlockSpec(memory_space=pltpu.VMEM)


def params(mib):
    return pltpu.CompilerParams(vmem_limit_bytes=mib * MIB)


def room(*arrays):
    total = 0
    for a in arrays:
        lanes = pl.cdiv(a.shape[-1], LANES) * LANES
        total += math.prod(a.shape[:-1]) * lanes * jnp.dtype(a.dtype).itemsize
    return params(total // MIB + 5)


def cost(flops, nbytes):
    return pl.CostEstimate(flops=int(flops), bytes_accessed=int(nbytes), transcendentals=0)


def struct(shape, dtype=jnp.bfloat16):
    return jax.ShapeDtypeStruct(shape, dtype)


def shift(x, count, by):
    return lax.ppermute(x, "tensor", [(i, (i + by) % count) for i in range(count)])


def hop(x, pairs):
    return lax.ppermute(x, "tensor", pairs)


def swap(x, count, mask):
    return lax.ppermute(x, "dp", [(i, i ^ mask) for i in range(count)])


def contract_rows(left, right):
    return lax.dot_general(
        left, right, (((0,), (0,)), ((), ())), preferred_element_type=jnp.float32
    )


def contract_cols(left, right):
    return lax.dot_general(
        left, right, (((1,), (1,)), ((), ())), preferred_element_type=jnp.float32
    )


def scaled_difference(student, projected, factor):
    wide = student.astype(jnp.float32) - projected.astype(jnp.float32)
    return (wide * factor).astype(jnp.bfloat16)


def prepare(row_map, teacher, mlp_input, student, projected, down, n_dp, n_t, factor):
    tok, width = mlp_input.shape
    rows = down.shape[0] // GROUP
    wide = teacher.shape[1] // n_dp
    hbm = pl.BlockSpec(memory_space=pltpu.HBM)
    if wide % LANES:
        blocks = teacher.reshape(tok, n_dp, wide).transpose(1, 0, 2)
        numbers = jnp.stack([row_map // LANES, row_map % LANES]).astype(jnp.bfloat16)
        numbers = jnp.broadcast_to(numbers.reshape(1, -1, wide), (n_dp, 2 * tok // wide, wide))
        blocks = jnp.concatenate([blocks, numbers], axis=1)
        wide = 0

    def kernel(m_ref, t_ref, x_ref, s_ref, p_ref, d_ref, own_ref, *refs):
        pieces, outs = refs[:n_t], refs[n_t:-4]
        s_buf, p_buf, m_buf, sems = refs[-4:]
        row = pl.multiple_of((lax.axis_index("dp") % GROUP) * rows, rows)
        pairs = [
            (s_ref.at[:, :PB], s_buf),
            (p_ref.at[:, :PB], p_buf),
            (m_ref, m_buf),
            (x_ref, own_ref.at[:, :width]),
        ]
        for k in range(n_t):
            col = pl.multiple_of(((lax.axis_index("tensor") + k) % n_t) * width, width)
            pairs.append((d_ref.at[pl.ds(row, rows), pl.ds(col, width)], pieces[k]))
        if wide:
            for i in range(n_dp):
                pairs.append((t_ref.at[:, i * wide : (i + 1) * wide], outs[0].at[i, :tok]))
        copies = [
            pltpu.make_async_copy(src, dst, sems.at[i]) for i, (src, dst) in enumerate(pairs)
        ]
        for c in copies:
            c.start()
        for c in copies[:3]:
            c.wait()
        own_ref[:, width:] = scaled_difference(s_buf[...], p_buf[...], factor)
        line = lax.broadcasted_iota(jnp.int32, (16, tok), 0)
        number = jnp.broadcast_to(m_buf[...], (16, tok))
        high, low = number // LANES, number % LANES
        digits = jnp.where(line == 0, high, jnp.where(line == 1, low, 0))
        digits = digits.astype(jnp.float32).astype(jnp.bfloat16)
        if wide:
            for i in range(n_dp):
                outs[0][i, tok:, :] = jnp.zeros((16, wide), jnp.bfloat16)
                outs[0][i, tok:, :tok] = digits
        for c in copies[3:]:
            c.wait()

    shapes = [(tok, width + PB)] + [(rows, width)] * n_t
    if wide:
        shapes.append((n_dp, tok + 16, wide))
    out = pl.pallas_call(
        kernel,
        in_specs=[hbm] * 6,
        out_specs=[VMEM] * len(shapes),
        out_shape=[struct(s) for s in shapes],
        scratch_shapes=[
            pltpu.VMEM((tok, PB), jnp.bfloat16),
            pltpu.VMEM((tok, PB), jnp.bfloat16),
            pltpu.VMEM((1, tok), jnp.int32),
            pltpu.SemaphoreType.DMA((4 + n_t + n_dp,)),
        ],
        compiler_params=params(60),
        cost_estimate=cost(0, 1024),
        name="prepare",
    )(row_map.reshape(1, tok), teacher, mlp_input, student, projected, down)
    return out if wide else [*out, blocks]


def stack_rows(parts, rows, width, after=()):
    def kernel(*refs):
        out_ref = refs[-1]
        for i, ref in enumerate(refs[: len(parts)]):
            out_ref[i * rows : (i + 1) * rows] = ref[ref.shape[0] - rows :, :width]

    return pl.pallas_call(
        kernel,
        in_specs=[VMEM] * len(parts) + [pl.BlockSpec(memory_space=pl.ANY)] * len(after),
        out_specs=VMEM,
        out_shape=struct((len(parts) * rows, width)),
        compiler_params=room(*parts),
        cost_estimate=cost(0, 1024),
        name="stack_rows",
    )(*parts, *after)


def ordered(x, *after):
    def kernel(*refs):
        pass

    return pl.pallas_call(
        kernel,
        in_specs=[pl.BlockSpec(memory_space=pl.ANY)] * (1 + len(after)),
        out_specs=pl.BlockSpec(memory_space=pl.ANY),
        out_shape=struct(x.shape, x.dtype),
        input_output_aliases={0: 0},
        compiler_params=params(1),
        cost_estimate=cost(0, 1024),
        name="ordered",
    )(x, *after)


def partial_products(near, far, student, projected, n_t, rows, factor, after):
    tok, width = student.shape
    hb = rows * GROUP
    half = GROUP // 2

    def kernel(near_ref, far_ref, s_ref, p_ref, *refs):
        outs = refs[len(after) :]
        err = scaled_difference(s_ref[...], p_ref[...], factor)
        place = lax.axis_index("dp") % GROUP
        for side, ref in enumerate((near_ref, far_ref)):
            product = contract_cols(ref[...], err)
            for j in range(half):
                row = pl.multiple_of((place ^ (2 * j + side)) * rows, rows)
                for k in range(n_t):
                    at = (j * n_t + k) * rows
                    outs[k][pl.ds(row, rows), :] = product[at : at + rows]

    return pl.pallas_call(
        kernel,
        in_specs=[VMEM] * 4
        + [pl.BlockSpec(memory_space=pl.ANY)] * len(after),
        out_specs=[VMEM] * n_t,
        out_shape=[struct((hb, tok), jnp.float32)] * n_t,
        compiler_params=room(near, near, far, student, projected, student),
        cost_estimate=cost(0, 1024),
        name="partial_products",
    )(near, far, student, projected, *after)


def weight_copies(gate_ref, up_ref, w_ref, sems, slots, width):
    hb = gate_ref.shape[1]
    copies = []
    for i, slot in enumerate(slots):
        at = pl.ds(pl.multiple_of(slot * width, width), width)
        for j, ref in enumerate((gate_ref, up_ref)):
            dst = w_ref.at[i, :, j * hb : (j + 1) * hb]
            copies.append(pltpu.make_async_copy(ref.at[at], dst, sems.at[2 * i + j]))
    return copies


def place_slices(slices, places, width, n_t, n_dp):
    count = slices[0].shape[0]
    cols = width * n_t // n_dp
    per = width // cols

    def kernel(*refs):
        out_ref = refs[-1]
        for k, x_ref in zip(places, refs):
            slot = (lax.axis_index("tensor") + n_t - k) % n_t
            for b in range(per):
                out_ref[slot * per + b, :, PB:] = x_ref[:, b * cols : (b + 1) * cols]

            @pl.when(slot == 0)
            def _(x_ref=x_ref):
                for i in range(n_dp):
                    out_ref[i, :, :PB] = x_ref[:, width:]

    return pl.pallas_call(
        kernel,
        in_specs=[VMEM] * len(slices),
        out_specs=VMEM,
        out_shape=struct((n_dp, count, PB + cols)),
        compiler_params=room(*slices, struct((n_dp, count, PB + cols))),
        cost_estimate=cost(0, 1024),
        name="place_slices",
    )(*slices)


def place_last(payload, from_left, from_right, ends, width, n_t, after=()):
    n_dp = payload.shape[0]
    cols = width * n_t // n_dp
    per = width // cols
    aligned = cols % LANES == 0
    hbm = pl.BlockSpec(memory_space=pltpu.HBM)

    def kernel(in_ref, left_ref, right_ref, last_ref, first_ref, *refs):
        out_ref, sems = refs[len(after) :]
        t = lax.axis_index("tensor")
        if not aligned:
            out_ref[...] = in_ref[...]

        def place(ref, slot):
            if not aligned:
                for b in range(per):
                    out_ref[slot * per + b, :, PB:] = ref[:, b * cols : (b + 1) * cols]

                @pl.when(slot == 0)
                def _():
                    for i in range(n_dp):
                        out_ref[i, :, :PB] = ref[:, width:]

                return
            copies = []
            for b in range(per):
                src = ref.at[:, pl.ds(b * cols, cols)]
                dst = out_ref.at[slot * per + b, :, pl.ds(PB, cols)]
                copies.append(pltpu.make_async_copy(src, dst, sems.at[b]))
            for c in copies:
                c.start()

            @pl.when(slot == 0)
            def _():
                extra = []
                for i in range(n_dp):
                    src = ref.at[:, pl.ds(width, PB)]
                    dst = out_ref.at[i, :, pl.ds(0, PB)]
                    extra.append(pltpu.make_async_copy(src, dst, sems.at[per + i]))
                for c in extra:
                    c.start()
                for c in extra:
                    c.wait()

            for c in copies:
                c.wait()

        half = n_t // 2
        for ref, slot, here in (
            (left_ref, t - half, t >= half),
            (right_ref, t + half, t < half),
            (last_ref, 0, t == n_t - 1),
            (first_ref, n_t - 1, t == 0),
        ):
            pl.when(here)(functools.partial(place, ref, slot))

    return pl.pallas_call(
        kernel,
        in_specs=[hbm if aligned else VMEM]
        + [VMEM] * 4
        + [pl.BlockSpec(memory_space=pl.ANY)] * len(after),
        out_specs=hbm if aligned else VMEM,
        out_shape=struct(payload.shape),
        input_output_aliases={0: 0} if aligned else {},
        scratch_shapes=[pltpu.SemaphoreType.DMA((per + n_dp,))],
        compiler_params=room(from_left, from_left, from_left, from_left, *([] if aligned else [payload] * 2)),
        cost_estimate=cost(0, 1024),
        name="place_last",
    )(payload, from_left, from_right, *ends, *after)


def gate_and_up(slices, gate, up, n_t, after):
    count, width, hb = slices[0].shape[0], gate.shape[0] // n_t, gate.shape[1]
    n_s = len(slices)

    def kernel(*refs):
        xs, gate_ref, up_ref = refs[:n_s], refs[n_s], refs[n_s + 1]
        pre_ref, w_ref, sems = refs[-3:]
        t = lax.axis_index("tensor")
        slots = [t, (t + n_t - 1) % n_t, (t + 1) % n_t, (t + n_t // 2) % n_t]
        copies = weight_copies(gate_ref, up_ref, w_ref, sems, slots, width)
        for c in copies:
            c.start()
        left = jnp.where(t == 0, xs[6][:, :width], xs[1][:, :width])
        right = jnp.where(t == n_t - 1, xs[5][:, :width], xs[2][:, :width])
        away = jnp.where(t < n_t // 2, xs[4][:, :width], xs[3][:, :width])
        pre = jnp.zeros((count, 2 * hb), jnp.float32)
        for i, x in enumerate([xs[0][:, :width], left, right, away]):
            copies[2 * i].wait()
            copies[2 * i + 1].wait()
            pre += jnp.dot(x, w_ref[i], preferred_element_type=jnp.float32)
        pre_ref[...] = pre

    return pl.pallas_call(
        kernel,
        in_specs=[VMEM] * n_s
        + [pl.BlockSpec(memory_space=pltpu.HBM)] * 2
        + [pl.BlockSpec(memory_space=pl.ANY)] * len(after),
        out_specs=VMEM,
        out_shape=struct((count, 2 * hb), jnp.float32),
        scratch_shapes=[
            pltpu.VMEM((n_t, width, 2 * hb), jnp.bfloat16),
            pltpu.SemaphoreType.DMA((2 * n_t,)),
        ],
        compiler_params=room(*slices, gate, up, *slices[:2]),
        cost_estimate=cost(0, 1024),
        name="gate_and_up",
    )(*slices, gate, up, *after)


def gradients(pre, acts):
    count, hb = pre.shape[0], pre.shape[1] // 2

    def kernel(pre_ref, *refs):
        act_refs, out_ref = refs[:-1], refs[-1]
        act = act_refs[0][...]
        for ref in act_refs[1:]:
            act += ref[...]
        act = act.T
        gate_pre, up_pre = pre_ref[:, :hb], pre_ref[:, hb:]
        s = jax.nn.sigmoid(gate_pre)
        gate_grad = act * up_pre * s * (1.0 + gate_pre * (1.0 - s))
        up_grad = act * gate_pre * s
        out_ref[:, :hb] = gate_grad.astype(jnp.bfloat16)
        out_ref[:, hb:] = up_grad.astype(jnp.bfloat16)

    return pl.pallas_call(
        kernel,
        in_specs=[VMEM] * (1 + len(acts)),
        out_specs=VMEM,
        out_shape=struct((count, 2 * hb)),
        compiler_params=room(pre, *acts, pre, pre, pre),
        cost_estimate=cost(0, 1024),
        name="gradients",
    )(pre, *acts)


def projector(came, teach, tok):
    n_dp, _, wide = teach.shape
    groups = n_dp // GROUP
    span = GROUP * tok
    digits = teach[:, tok:]
    if wide < tok:
        digits = digits.reshape(n_dp, 2, tok)
        digits = jnp.pad(digits, ((0, 0), (0, 14), (0, 0)))
        teach = teach[:, :tok]

    def kernel(came_ref, teach_ref, digits_ref, out_ref, flipped_ref):
        def flip(g, carry):
            bucket = came_ref[pl.ds(g * GROUP, GROUP), :, :PB].reshape(span, PB)
            flipped_ref[g] = bucket.astype(jnp.float32).T.astype(jnp.bfloat16)
            return carry

        lax.fori_loop(0, groups, flip, 0)
        out_ref[...] = jnp.zeros_like(out_ref)

        def sender(g, carry):
            lines = digits_ref[g, :, :tok].astype(jnp.float32)
            number = (lines[0:1] * float(LANES) + lines[1:2]).astype(jnp.int32)

            def block(h, total):
                token = lax.broadcasted_iota(jnp.int32, (span, tok), 0) + h * span
                picks = (token == number).astype(jnp.float32).astype(jnp.bfloat16)
                return total + jnp.dot(flipped_ref[h], picks, preferred_element_type=jnp.float32)

            rows = lax.fori_loop(0, groups, block, jnp.zeros((PB, tok), jnp.float32))
            out_ref[...] += jnp.dot(
                rows.astype(jnp.bfloat16), teach_ref[g, :tok], preferred_element_type=jnp.float32
            )
            return carry

        lax.fori_loop(0, n_dp, sender, 0)

    return pl.pallas_call(
        kernel,
        in_specs=[VMEM] * 3,
        out_specs=VMEM,
        out_shape=struct((PB, wide), jnp.float32),
        scratch_shapes=[pltpu.VMEM((groups, PB, span), jnp.bfloat16)],
        compiler_params=params(24),
        cost_estimate=cost(0, 1024),
        name="projector",
    )(came, teach, digits)


def final_product(feats, grads, masks):
    n_dp, count = feats.shape[:2]
    hb, cols = grads[0].shape[-1] // 2, feats.shape[2] - PB

    def kernel(feats_ref, *refs):
        grad_refs, (gate_ref, up_ref) = refs[: len(grads)], refs[len(grads) : len(grads) + 2]

        def group(g, total):
            here = pl.ds(g * GROUP, GROUP)
            left = left_ref[here].reshape(GROUP * count, 2 * hb)
            right = feats_ref[here, :, PB:].reshape(GROUP * count, cols)
            return total + contract_rows(left, right)

        total = jnp.zeros((2 * hb, cols), jnp.float32)
        if masks:
            left_ref = refs[-1]
            for mask, ref in zip(masks, grad_refs):
                left_ref[lax.axis_index("dp") ^ mask] = ref[...]
            total = group(0, total)
        else:
            left_ref = grad_refs[0]
            total = lax.fori_loop(0, n_dp // GROUP, group, total)
        gate_ref[...] = total[:hb]
        up_ref[...] = total[hb:]

    return pl.pallas_call(
        kernel,
        in_specs=[VMEM] * (1 + len(grads)),
        out_specs=[VMEM] * 2,
        out_shape=[struct((hb, cols), jnp.float32)] * 2,
        scratch_shapes=[pltpu.VMEM((n_dp, count, 2 * hb), jnp.bfloat16)] if masks else [],
        compiler_params=params(40),
        cost_estimate=cost(0, 1024),
        name="final_product",
    )(feats, *grads)


def body(
    teacher_rows, row_map, student_hidden, projected, mlp_input, gate_bucket, up_bucket, down_bucket
):
    tok = row_map.shape[0]
    n_dp = lax.axis_size("dp")
    n_t = lax.axis_size("tensor")
    hb, width = down_bucket.shape[0], student_hidden.shape[1]
    cols = width * n_t // n_dp
    factor = 1.0 / math.sqrt(tok * n_dp)
    rows = hb // GROUP

    own, *pieces, teach = prepare(
        row_map, teacher_rows, mlp_input, student_hidden, projected, down_bucket, n_dp, n_t, factor
    )
    rightward = [(i, i + 1) for i in range(n_t - 1)]
    leftward = [(i + 1, i) for i in range(n_t - 1)]
    teach = lax.all_to_all(teach, "dp", split_axis=0, concat_axis=0, tiled=True)
    from_left, from_right = hop(own, rightward), hop(own, leftward)
    mine = stack_rows(
        [pieces[0]] + [shift(pieces[k], n_t, k) for k in range(1, n_t)], rows, width
    )
    others = [swap(mine, n_dp, mask) for mask in (2, 4, 6)]

    from_left, from_right = ordered(from_left, mine), ordered(from_right, mine)
    far_left, far_right = hop(from_left, rightward[1:]), hop(from_right, leftward[:-1])
    ends = [hop(far_left, rightward[-1:]), hop(far_right, leftward[:1])]

    near = stack_rows([mine] + others, n_t * rows, width, after=[teach])
    far = swap(near, n_dp, 1)
    partial = partial_products(near, far, student_hidden, projected, n_t, rows, factor, after=[])
    acts = [partial[0]] + [shift(partial[k], n_t, -k) for k in range(1, n_t)]

    sent = place_slices([own, from_left, from_right], [0, 1, n_t - 1], width, n_t, n_dp)
    sent = place_last(sent, far_left, far_right, ends, width, n_t, after=[partial[0]])
    feats = lax.all_to_all(sent, "dp", split_axis=0, concat_axis=0, tiled=True)

    slices = [own, from_left, from_right, far_left, far_right, *ends]
    pre = gate_and_up(slices, gate_bucket, up_bucket, n_t, after=[sent])
    grads = gradients(pre, acts)
    masks = list(range(n_dp)) if n_dp == GROUP else []
    if masks:
        grads = [grads] + [swap(grads, n_dp, mask) for mask in masks[1:]]
    else:
        grads = [lax.all_gather(grads, "dp")]
    grad_proj = projector(feats, teach, tok)
    grad_gate, grad_up = final_product(feats, grads, masks)
    return (grad_proj[:, None, :], grad_gate, grad_up)


def solution(mesh):
    in_specs = (
        P("dp", "tensor"),
        P("dp"),
        P("dp", "tensor"),
        P("dp", "tensor"),
        P("dp", "tensor"),
        P(None, "tensor"),
        P(None, "tensor"),
        P("tensor", None),
    )
    out_specs = (P(None, "tensor", "dp"), P("tensor", "dp"), P("tensor", "dp"))
    return jax.shard_map(body, mesh=mesh, in_specs=in_specs, out_specs=out_specs, check_vma=False)
```

```python
import functools
import math

import jax
import jax.numpy as jnp
from jax import lax
from jax.experimental import pallas as pl
from jax.experimental.pallas import tpu as pltpu
from jax.sharding import PartitionSpec as P

PB = 128
LANES = 128
GROUP = 8
MIB = 1 << 20

VMEM = pl.BlockSpec(memory_space=pltpu.VMEM)


def params(mib):
    return pltpu.CompilerParams(vmem_limit_bytes=mib * MIB)


def cost(flops, nbytes):
    return pl.CostEstimate(flops=int(flops), bytes_accessed=int(nbytes), transcendentals=0)


def struct(shape, dtype=jnp.bfloat16):
    return jax.ShapeDtypeStruct(shape, dtype)


def shift(x, count, by):
    return lax.ppermute(x, "tensor", [(i, (i + by) % count) for i in range(count)])


def hop(x, pairs):
    return lax.ppermute(x, "tensor", pairs)


def swap(x, count, mask):
    return lax.ppermute(x, "dp", [(i, i ^ mask) for i in range(count)])


def contract_rows(left, right):
    return lax.dot_general(
        left, right, (((0,), (0,)), ((), ())), preferred_element_type=jnp.float32
    )


def contract_cols(left, right):
    return lax.dot_general(
        left, right, (((1,), (1,)), ((), ())), preferred_element_type=jnp.float32
    )


def scaled_difference(student, projected, factor):
    wide = student.astype(jnp.float32) - projected.astype(jnp.float32)
    return (wide * factor).astype(jnp.bfloat16)


def prepare(row_map, teacher, mlp_input, student, projected, down, n_dp, n_t, factor):
    tok, width = mlp_input.shape
    rows = down.shape[0] // GROUP
    wide = teacher.shape[1] // n_dp
    hbm = pl.BlockSpec(memory_space=pltpu.HBM)
    if wide % LANES:
        blocks = teacher.reshape(tok, n_dp, wide).transpose(1, 0, 2)
        numbers = jnp.stack([row_map // LANES, row_map % LANES]).astype(jnp.bfloat16)
        numbers = jnp.broadcast_to(numbers.reshape(1, -1, wide), (n_dp, 2 * tok // wide, wide))
        blocks = jnp.concatenate([blocks, numbers], axis=1)
        wide = 0

    def kernel(m_ref, t_ref, x_ref, s_ref, p_ref, d_ref, own_ref, *refs):
        pieces, outs = refs[:n_t], refs[n_t:-4]
        s_buf, p_buf, m_buf, sems = refs[-4:]
        row = pl.multiple_of((lax.axis_index("dp") % GROUP) * rows, rows)
        pairs = [
            (s_ref.at[:, :PB], s_buf),
            (p_ref.at[:, :PB], p_buf),
            (m_ref, m_buf),
            (x_ref, own_ref.at[:, :width]),
        ]
        for k in range(n_t):
            col = pl.multiple_of(((lax.axis_index("tensor") + k) % n_t) * width, width)
            pairs.append((d_ref.at[pl.ds(row, rows), pl.ds(col, width)], pieces[k]))
        if wide:
            for i in range(n_dp):
                pairs.append((t_ref.at[:, i * wide : (i + 1) * wide], outs[0].at[i, :tok]))
        copies = [
            pltpu.make_async_copy(src, dst, sems.at[i]) for i, (src, dst) in enumerate(pairs)
        ]
        for c in copies:
            c.start()
        for c in copies[:3]:
            c.wait()
        own_ref[:, width:] = scaled_difference(s_buf[...], p_buf[...], factor)
        line = lax.broadcasted_iota(jnp.int32, (16, tok), 0)
        number = jnp.broadcast_to(m_buf[...], (16, tok))
        high, low = number // LANES, number % LANES
        digits = jnp.where(line == 0, high, jnp.where(line == 1, low, 0))
        digits = digits.astype(jnp.float32).astype(jnp.bfloat16)
        if wide:
            for i in range(n_dp):
                outs[0][i, tok:, :] = jnp.zeros((16, wide), jnp.bfloat16)
                outs[0][i, tok:, :tok] = digits
        for c in copies[3:]:
            c.wait()

    shapes = [(tok, width + PB)] + [(rows, width)] * n_t
    if wide:
        shapes.append((n_dp, tok + 16, wide))
    out = pl.pallas_call(
        kernel,
        in_specs=[hbm] * 6,
        out_specs=[VMEM] * len(shapes),
        out_shape=[struct(s) for s in shapes],
        scratch_shapes=[
            pltpu.VMEM((tok, PB), jnp.bfloat16),
            pltpu.VMEM((tok, PB), jnp.bfloat16),
            pltpu.VMEM((1, tok), jnp.int32),
            pltpu.SemaphoreType.DMA((4 + n_t + n_dp,)),
        ],
        compiler_params=params(60),
        cost_estimate=cost(0, 1024),
        name="prepare",
    )(row_map.reshape(1, tok), teacher, mlp_input, student, projected, down)
    return out if wide else [*out, blocks]


def stack_rows(parts, rows, width, mib, after=()):
    def kernel(*refs):
        out_ref = refs[-1]
        for i, ref in enumerate(refs[: len(parts)]):
            out_ref[i * rows : (i + 1) * rows] = ref[ref.shape[0] - rows :, :width]

    return pl.pallas_call(
        kernel,
        in_specs=[VMEM] * len(parts) + [pl.BlockSpec(memory_space=pl.ANY)] * len(after),
        out_specs=VMEM,
        out_shape=struct((len(parts) * rows, width)),
        compiler_params=params(mib),
        cost_estimate=cost(0, 1024),
        name="stack_rows",
    )(*parts, *after)


def ordered(x, *after):
    def kernel(*refs):
        pass

    return pl.pallas_call(
        kernel,
        in_specs=[pl.BlockSpec(memory_space=pl.ANY)] * (1 + len(after)),
        out_specs=pl.BlockSpec(memory_space=pl.ANY),
        out_shape=struct(x.shape, x.dtype),
        input_output_aliases={0: 0},
        compiler_params=params(1),
        cost_estimate=cost(0, 1024),
        name="ordered",
    )(x, *after)


def partial_products(near, far, student, projected, n_t, rows, factor, after):
    tok, width = student.shape
    hb = rows * GROUP
    half = GROUP // 2

    def kernel(near_ref, far_ref, s_ref, p_ref, *refs):
        outs = refs[len(after) :]
        err = scaled_difference(s_ref[...], p_ref[...], factor)
        place = lax.axis_index("dp") % GROUP
        for side, ref in enumerate((near_ref, far_ref)):
            product = contract_cols(ref[...], err)
            for j in range(half):
                row = pl.multiple_of((place ^ (2 * j + side)) * rows, rows)
                for k in range(n_t):
                    at = (j * n_t + k) * rows
                    outs[k][pl.ds(row, rows), :] = product[at : at + rows]

    return pl.pallas_call(
        kernel,
        in_specs=[VMEM] * 4
        + [pl.BlockSpec(memory_space=pl.ANY)] * len(after),
        out_specs=[VMEM] * n_t,
        out_shape=[struct((hb, tok), jnp.float32)] * n_t,
        compiler_params=params(60),
        cost_estimate=cost(0, 1024),
        name="partial_products",
    )(near, far, student, projected, *after)


def weight_copies(gate_ref, up_ref, w_ref, sems, slots, width):
    hb = gate_ref.shape[1]
    copies = []
    for i, slot in enumerate(slots):
        at = pl.ds(pl.multiple_of(slot * width, width), width)
        for j, ref in enumerate((gate_ref, up_ref)):
            dst = w_ref.at[i, :, j * hb : (j + 1) * hb]
            copies.append(pltpu.make_async_copy(ref.at[at], dst, sems.at[2 * i + j]))
    return copies


def place_slices(slices, places, width, n_t, n_dp):
    count = slices[0].shape[0]
    cols = width * n_t // n_dp
    per = width // cols

    def kernel(*refs):
        out_ref = refs[-1]
        for k, x_ref in zip(places, refs):
            slot = (lax.axis_index("tensor") + n_t - k) % n_t
            for b in range(per):
                out_ref[slot * per + b] = x_ref[:, b * cols : (b + 1) * cols]

    return pl.pallas_call(
        kernel,
        in_specs=[VMEM] * len(slices),
        out_specs=VMEM,
        out_shape=struct((n_dp, count, cols)),
        compiler_params=params(60),
        cost_estimate=cost(0, 1024),
        name="place_slices",
    )(*slices)


def place_last(payload, from_left, from_right, ends, width, n_t, after=()):
    n_dp = payload.shape[0]
    cols = width * n_t // n_dp
    per = width // cols
    aligned = cols % LANES == 0
    hbm = pl.BlockSpec(memory_space=pltpu.HBM)

    def kernel(in_ref, left_ref, right_ref, last_ref, first_ref, *refs):
        out_ref, sems = refs[len(after) :]
        t = lax.axis_index("tensor")
        if not aligned:
            out_ref[...] = in_ref[...]

        def place(ref, slot):
            if not aligned:
                for b in range(per):
                    out_ref[slot * per + b] = ref[:, b * cols : (b + 1) * cols]
                return
            copies = []
            for b in range(per):
                src = ref.at[:, pl.ds(b * cols, cols)]
                dst = out_ref.at[slot * per + b]
                copies.append(pltpu.make_async_copy(src, dst, sems.at[b]))
            for c in copies:
                c.start()

            for c in copies:
                c.wait()

        half = n_t // 2
        for ref, slot, here in (
            (left_ref, t - half, t >= half),
            (right_ref, t + half, t < half),
            (last_ref, 0, t == n_t - 1),
            (first_ref, n_t - 1, t == 0),
        ):
            pl.when(here)(functools.partial(place, ref, slot))

    return pl.pallas_call(
        kernel,
        in_specs=[hbm if aligned else VMEM]
        + [VMEM] * 4
        + [pl.BlockSpec(memory_space=pl.ANY)] * len(after),
        out_specs=hbm if aligned else VMEM,
        out_shape=struct(payload.shape),
        input_output_aliases={0: 0} if aligned else {},
        scratch_shapes=[pltpu.SemaphoreType.DMA((per,))],
        compiler_params=params(60),
        cost_estimate=cost(0, 1024),
        name="place_last",
    )(payload, from_left, from_right, *ends, *after)


def gate_and_up(slices, gate, up, n_t, after):
    count, width, hb = slices[0].shape[0], gate.shape[0] // n_t, gate.shape[1]
    n_s = len(slices)

    def kernel(*refs):
        xs, gate_ref, up_ref = refs[:n_s], refs[n_s], refs[n_s + 1]
        pre_ref, w_ref, sems = refs[-3:]
        t = lax.axis_index("tensor")
        slots = [t, (t + n_t - 1) % n_t, (t + 1) % n_t, (t + n_t // 2) % n_t]
        copies = weight_copies(gate_ref, up_ref, w_ref, sems, slots, width)
        for c in copies:
            c.start()
        left = jnp.where(t == 0, xs[6][:, :width], xs[1][:, :width])
        right = jnp.where(t == n_t - 1, xs[5][:, :width], xs[2][:, :width])
        away = jnp.where(t < n_t // 2, xs[4][:, :width], xs[3][:, :width])
        pre = jnp.zeros((count, 2 * hb), jnp.float32)
        for i, x in enumerate([xs[0][:, :width], left, right, away]):
            copies[2 * i].wait()
            copies[2 * i + 1].wait()
            pre += jnp.dot(x, w_ref[i], preferred_element_type=jnp.float32)
        pre_ref[...] = pre

    return pl.pallas_call(
        kernel,
        in_specs=[VMEM] * n_s
        + [pl.BlockSpec(memory_space=pltpu.HBM)] * 2
        + [pl.BlockSpec(memory_space=pl.ANY)] * len(after),
        out_specs=VMEM,
        out_shape=struct((count, 2 * hb), jnp.float32),
        scratch_shapes=[
            pltpu.VMEM((n_t, width, 2 * hb), jnp.bfloat16),
            pltpu.SemaphoreType.DMA((2 * n_t,)),
        ],
        compiler_params=params(60),
        cost_estimate=cost(0, 1024),
        name="gate_and_up",
    )(*slices, gate, up, *after)


def gradients(pre, acts, slices, width):
    count, hb = pre.shape[0], pre.shape[1] // 2

    def kernel(pre_ref, *refs):
        act_refs, xs, out_ref = refs[: len(acts)], refs[len(acts) : -1], refs[-1]
        act = act_refs[0][...]
        for ref in act_refs[1:]:
            act += ref[...]
        act = act.T
        gate_pre, up_pre = pre_ref[:, :hb], pre_ref[:, hb:]
        s = jax.nn.sigmoid(gate_pre)
        gate_grad = act * up_pre * s * (1.0 + gate_pre * (1.0 - s))
        up_grad = act * gate_pre * s
        out_ref[:, :hb] = gate_grad.astype(jnp.bfloat16)
        out_ref[:, hb : 2 * hb] = up_grad.astype(jnp.bfloat16)
        for i, ref in enumerate(xs):

            @pl.when(lax.axis_index("tensor") == i)
            def _(ref=ref):
                out_ref[:, 2 * hb :] = ref[...]

    bucket = pl.BlockSpec((count, PB), lambda i: (0, width // PB))

    def whole(x):
        return pl.BlockSpec(x.shape, lambda i: (0, 0))

    return pl.pallas_call(
        kernel,
        grid=(1,),
        in_specs=[whole(x) for x in (pre, *acts)] + [bucket] * len(slices),
        out_specs=pl.BlockSpec((count, 2 * hb + PB), lambda i: (0, 0)),
        out_shape=struct((count, 2 * hb + PB)),
        compiler_params=params(60),
        cost_estimate=cost(0, 1024),
        name="gradients",
    )(pre, *acts, *slices)


def hand_over(teach, tok, after):
    n_dp, _, wide = teach.shape
    groups = n_dp // GROUP
    span = GROUP * tok
    digits = []
    if wide < tok:
        digits = teach[:, tok:].reshape(n_dp, 2, tok)
        digits = [jnp.pad(digits, ((0, 0), (0, 14), (0, 0)))]

    def kernel(*refs):
        teach_ref, (out_ref, total_ref) = refs[0], refs[-2:]

        def receivers(h, carry):
            total_ref[...] = jnp.zeros_like(total_ref)

            def sender(g, carry):
                lines = refs[1][g] if digits else teach_ref[g, tok : tok + 16, :tok]
                lines = lines.astype(jnp.float32)
                number = (lines[0:1] * float(LANES) + lines[1:2]).astype(jnp.int32)
                token = lax.broadcasted_iota(jnp.int32, (span, tok), 0) + h * span
                picks = (token == number).astype(jnp.float32).astype(jnp.bfloat16)
                total_ref[...] += jnp.dot(
                    picks, teach_ref[g, :tok], preferred_element_type=jnp.float32
                )
                return carry

            lax.fori_loop(0, n_dp, sender, 0)
            out_ref[pl.ds(h * GROUP, GROUP)] = (
                total_ref[...].astype(jnp.bfloat16).reshape(GROUP, tok, wide)
            )
            return carry

        lax.fori_loop(0, groups, receivers, 0)

    return pl.pallas_call(
        kernel,
        in_specs=[VMEM] * (1 + len(digits)) + [pl.BlockSpec(memory_space=pl.ANY)] * len(after),
        out_specs=VMEM,
        out_shape=struct((n_dp, tok, wide)),
        scratch_shapes=[pltpu.VMEM((span, wide), jnp.float32)],
        compiler_params=params(60),
        cost_estimate=cost(0, 1024),
        name="hand_over",
    )(teach, *digits, *after)


def final_product(feats, handed, grads, masks):
    n_dp, count, cols = feats.shape
    wide = handed.shape[2]
    hb = (grads[0].shape[-1] - PB) // 2

    def kernel(feats_ref, handed_ref, *refs):
        grad_refs, (proj_ref, gate_ref, up_ref) = refs[: len(grads)], refs[len(grads) : len(grads) + 3]

        def group(g, totals):
            here = pl.ds(g * GROUP, GROUP)
            left = left_ref[here].reshape(GROUP * count, 2 * hb + PB)
            right = feats_ref[here].reshape(GROUP * count, cols)
            rows = handed_ref[here].reshape(GROUP * count, wide)
            return (
                totals[0] + contract_rows(left[:, : 2 * hb], right),
                totals[1] + contract_rows(left[:, 2 * hb :], rows),
            )

        totals = (jnp.zeros((2 * hb, cols), jnp.float32), jnp.zeros((PB, wide), jnp.float32))
        if masks:
            left_ref = refs[-1]
            for mask, ref in zip(masks, grad_refs):
                left_ref[lax.axis_index("dp") ^ mask] = ref[...]
            totals = group(0, totals)
        else:
            left_ref = grad_refs[0]
            totals = lax.fori_loop(0, n_dp // GROUP, group, totals)
        gate_ref[...] = totals[0][:hb]
        up_ref[...] = totals[0][hb:]
        proj_ref[...] = totals[1].reshape(PB, 1, wide)

    return pl.pallas_call(
        kernel,
        in_specs=[VMEM] * (2 + len(grads)),
        out_specs=[VMEM] * 3,
        out_shape=[struct((PB, 1, wide), jnp.float32)] + [struct((hb, cols), jnp.float32)] * 2,
        scratch_shapes=[pltpu.VMEM((n_dp, count, 2 * hb + PB), jnp.bfloat16)] if masks else [],
        compiler_params=params(40),
        cost_estimate=cost(0, 1024),
        name="final_product",
    )(feats, handed, *grads)


def body(
    teacher_rows, row_map, student_hidden, projected, mlp_input, gate_bucket, up_bucket, down_bucket
):
    tok = row_map.shape[0]
    n_dp = lax.axis_size("dp")
    n_t = lax.axis_size("tensor")
    hb, width = down_bucket.shape[0], student_hidden.shape[1]
    cols = width * n_t // n_dp
    factor = 1.0 / math.sqrt(tok * n_dp)
    rows = hb // GROUP

    own, *pieces, teach = prepare(
        row_map, teacher_rows, mlp_input, student_hidden, projected, down_bucket, n_dp, n_t, factor
    )
    rightward = [(i, i + 1) for i in range(n_t - 1)]
    leftward = [(i + 1, i) for i in range(n_t - 1)]
    teach = lax.all_to_all(teach, "dp", split_axis=0, concat_axis=0, tiled=True)
    from_left, from_right = hop(own, rightward), hop(own, leftward)
    mine = stack_rows(
        [pieces[0]] + [shift(pieces[k], n_t, k) for k in range(1, n_t)], rows, width, 8
    )
    others = [swap(mine, n_dp, mask) for mask in (2, 4, 6)]

    from_left, from_right = ordered(from_left, mine), ordered(from_right, mine)
    far_left, far_right = hop(from_left, rightward[1:]), hop(from_right, leftward[:-1])
    ends = [hop(far_left, rightward[-1:]), hop(far_right, leftward[:1])]

    near = stack_rows(
        [mine] + others, n_t * rows, width, 60, after=[teach, far_left, far_right]
    )
    far = swap(near, n_dp, 1)
    partial = partial_products(near, far, student_hidden, projected, n_t, rows, factor, after=[])
    acts = [partial[0]] + [shift(partial[k], n_t, -k) for k in range(1, n_t)]

    sent = place_slices([own, from_left, from_right], [0, 1, n_t - 1], width, n_t, n_dp)
    sent = place_last(sent, far_left, far_right, ends, width, n_t, after=[partial[0]])
    feats = lax.all_to_all(sent, "dp", split_axis=0, concat_axis=0, tiled=True)

    slices = [own, from_left, from_right, far_left, far_right, *ends]
    pre = gate_and_up(slices, gate_bucket, up_bucket, n_t, after=[sent])
    grads = gradients(pre, acts, [own, from_left, far_left, ends[0]], width)
    masks = list(range(n_dp)) if n_dp == GROUP else []
    if masks:
        grads = [grads] + [swap(grads, n_dp, mask) for mask in masks[1:]]
    else:
        grads = [lax.all_gather(grads, "dp")]
    handed = hand_over(teach, tok, after=[sent])
    return final_product(feats, handed, grads, masks)


def solution(mesh):
    in_specs = (
        P("dp", "tensor"),
        P("dp"),
        P("dp", "tensor"),
        P("dp", "tensor"),
        P("dp", "tensor"),
        P(None, "tensor"),
        P(None, "tensor"),
        P("tensor", None),
    )
    out_specs = (P(None, "tensor", "dp"), P("tensor", "dp"), P("tensor", "dp"))
    return jax.shard_map(body, mesh=mesh, in_specs=in_specs, out_specs=out_specs, check_vma=False)
```

```python
import functools
import math

import jax
import jax.numpy as jnp
from jax import lax
from jax.experimental import pallas as pl
from jax.experimental.pallas import tpu as pltpu
from jax.sharding import PartitionSpec as P

PB = 128
LANES = 128
GROUP = 8
MIB = 1 << 20

VMEM = pl.BlockSpec(memory_space=pltpu.VMEM)


def params(mib):
    return pltpu.CompilerParams(vmem_limit_bytes=mib * MIB)


def cost(flops, nbytes):
    return pl.CostEstimate(flops=int(flops), bytes_accessed=int(nbytes), transcendentals=0)


def struct(shape, dtype=jnp.bfloat16):
    return jax.ShapeDtypeStruct(shape, dtype)


def shift(x, count, by):
    return lax.ppermute(x, "tensor", [(i, (i + by) % count) for i in range(count)])


def hop(x, pairs):
    return lax.ppermute(x, "tensor", pairs)


def swap(x, count, mask):
    return lax.ppermute(x, "dp", [(i, i ^ mask) for i in range(count)])


def contract_rows(left, right):
    return lax.dot_general(
        left, right, (((0,), (0,)), ((), ())), preferred_element_type=jnp.float32
    )


def contract_cols(left, right):
    return lax.dot_general(
        left, right, (((1,), (1,)), ((), ())), preferred_element_type=jnp.float32
    )


def scaled_difference(student, projected, factor):
    wide = student.astype(jnp.float32) - projected.astype(jnp.float32)
    return (wide * factor).astype(jnp.bfloat16)


def prepare(row_map, teacher, mlp_input, student, projected, down, n_dp, n_t, factor):
    tok, width = mlp_input.shape
    rows = down.shape[0] // GROUP
    wide = teacher.shape[1] // n_dp
    hbm = pl.BlockSpec(memory_space=pltpu.HBM)
    if wide % LANES:
        blocks = teacher.reshape(tok, n_dp, wide).transpose(1, 0, 2)
        numbers = jnp.stack([row_map // LANES, row_map % LANES]).astype(jnp.bfloat16)
        numbers = jnp.broadcast_to(numbers.reshape(1, -1, wide), (n_dp, 2 * tok // wide, wide))
        blocks = jnp.concatenate([blocks, numbers], axis=1)
        wide = 0

    def kernel(m_ref, t_ref, x_ref, s_ref, p_ref, d_ref, own_ref, *refs):
        pieces, outs = refs[:n_t], refs[n_t:-4]
        s_buf, p_buf, m_buf, sems = refs[-4:]
        row = pl.multiple_of((lax.axis_index("dp") % GROUP) * rows, rows)
        pairs = [
            (s_ref.at[:, :PB], s_buf),
            (p_ref.at[:, :PB], p_buf),
            (m_ref, m_buf),
            (x_ref, own_ref.at[:, :width]),
        ]
        for k in range(n_t):
            col = pl.multiple_of(((lax.axis_index("tensor") + k) % n_t) * width, width)
            pairs.append((d_ref.at[pl.ds(row, rows), pl.ds(col, width)], pieces[k]))
        if wide:
            for i in range(n_dp):
                pairs.append((t_ref.at[:, i * wide : (i + 1) * wide], outs[0].at[i, :tok]))
        copies = [
            pltpu.make_async_copy(src, dst, sems.at[i]) for i, (src, dst) in enumerate(pairs)
        ]
        for c in copies:
            c.start()
        for c in copies[:3]:
            c.wait()
        own_ref[:, width:] = scaled_difference(s_buf[...], p_buf[...], factor)
        line = lax.broadcasted_iota(jnp.int32, (16, tok), 0)
        number = jnp.broadcast_to(m_buf[...], (16, tok))
        high, low = number // LANES, number % LANES
        digits = jnp.where(line == 0, high, jnp.where(line == 1, low, 0))
        digits = digits.astype(jnp.float32).astype(jnp.bfloat16)
        if wide:
            for i in range(n_dp):
                outs[0][i, tok:, :] = jnp.zeros((16, wide), jnp.bfloat16)
                outs[0][i, tok:, :tok] = digits
        for c in copies[3:]:
            c.wait()

    shapes = [(tok, width + PB)] + [(rows, width)] * n_t
    if wide:
        shapes.append((n_dp, tok + 16, wide))
    out = pl.pallas_call(
        kernel,
        in_specs=[hbm] * 6,
        out_specs=[VMEM] * len(shapes),
        out_shape=[struct(s) for s in shapes],
        scratch_shapes=[
            pltpu.VMEM((tok, PB), jnp.bfloat16),
            pltpu.VMEM((tok, PB), jnp.bfloat16),
            pltpu.VMEM((1, tok), jnp.int32),
            pltpu.SemaphoreType.DMA((4 + n_t + n_dp,)),
        ],
        compiler_params=params(60),
        cost_estimate=cost(0, 1024),
        name="prepare",
    )(row_map.reshape(1, tok), teacher, mlp_input, student, projected, down)
    return out if wide else [*out, blocks]


def stack_rows(parts, rows, width, mib, after=()):
    def kernel(*refs):
        out_ref = refs[-1]
        for i, ref in enumerate(refs[: len(parts)]):
            out_ref[i * rows : (i + 1) * rows] = ref[ref.shape[0] - rows :, :width]

    return pl.pallas_call(
        kernel,
        in_specs=[VMEM] * len(parts) + [pl.BlockSpec(memory_space=pl.ANY)] * len(after),
        out_specs=VMEM,
        out_shape=struct((len(parts) * rows, width)),
        compiler_params=params(mib),
        cost_estimate=cost(0, 1024),
        name="stack_rows",
    )(*parts, *after)


def ordered(x, *after):
    def kernel(*refs):
        pass

    return pl.pallas_call(
        kernel,
        in_specs=[pl.BlockSpec(memory_space=pl.ANY)] * (1 + len(after)),
        out_specs=pl.BlockSpec(memory_space=pl.ANY),
        out_shape=struct(x.shape, x.dtype),
        input_output_aliases={0: 0},
        compiler_params=params(1),
        cost_estimate=cost(0, 1024),
        name="ordered",
    )(x, *after)


def partial_products(near, far, student, projected, n_t, rows, factor, after):
    tok, width = student.shape
    hb = rows * GROUP
    half = GROUP // 2

    def kernel(near_ref, far_ref, s_ref, p_ref, *refs):
        outs = refs[len(after) :]
        err = scaled_difference(s_ref[...], p_ref[...], factor)
        place = lax.axis_index("dp") % GROUP
        for side, ref in enumerate((near_ref, far_ref)):
            product = contract_cols(ref[...], err)
            for j in range(half):
                row = pl.multiple_of((place ^ (2 * j + side)) * rows, rows)
                for k in range(n_t):
                    at = (j * n_t + k) * rows
                    outs[k][pl.ds(row, rows), :] = product[at : at + rows]

    return pl.pallas_call(
        kernel,
        in_specs=[VMEM] * 4
        + [pl.BlockSpec(memory_space=pl.ANY)] * len(after),
        out_specs=[VMEM] * n_t,
        out_shape=[struct((hb, tok), jnp.float32)] * n_t,
        compiler_params=params(60),
        cost_estimate=cost(0, 1024),
        name="partial_products",
    )(near, far, student, projected, *after)


def weight_copies(gate_ref, up_ref, w_ref, sems, slots, width):
    hb = gate_ref.shape[1]
    copies = []
    for i, slot in enumerate(slots):
        at = pl.ds(pl.multiple_of(slot * width, width), width)
        for j, ref in enumerate((gate_ref, up_ref)):
            dst = w_ref.at[i, :, j * hb : (j + 1) * hb]
            copies.append(pltpu.make_async_copy(ref.at[at], dst, sems.at[2 * i + j]))
    return copies


def place_slices(slices, places, width, n_t, n_dp):
    count = slices[0].shape[0]
    cols = width * n_t // n_dp
    per = width // cols

    def kernel(*refs):
        out_ref = refs[-1]
        for k, x_ref in zip(places, refs):
            slot = (lax.axis_index("tensor") + n_t - k) % n_t
            for b in range(per):
                out_ref[slot * per + b] = x_ref[:, b * cols : (b + 1) * cols]

    return pl.pallas_call(
        kernel,
        in_specs=[VMEM] * len(slices),
        out_specs=VMEM,
        out_shape=struct((n_dp, count, cols)),
        compiler_params=params(60),
        cost_estimate=cost(0, 1024),
        name="place_slices",
    )(*slices)


def place_last(payload, from_left, from_right, ends, width, n_t, after=()):
    n_dp = payload.shape[0]
    cols = width * n_t // n_dp
    per = width // cols
    aligned = cols % LANES == 0
    hbm = pl.BlockSpec(memory_space=pltpu.HBM)

    def kernel(in_ref, left_ref, right_ref, last_ref, first_ref, *refs):
        out_ref, sems = refs[len(after) :]
        t = lax.axis_index("tensor")
        if not aligned:
            out_ref[...] = in_ref[...]

        def place(ref, slot):
            if not aligned:
                for b in range(per):
                    out_ref[slot * per + b] = ref[:, b * cols : (b + 1) * cols]
                return
            copies = []
            for b in range(per):
                src = ref.at[:, pl.ds(b * cols, cols)]
                dst = out_ref.at[slot * per + b]
                copies.append(pltpu.make_async_copy(src, dst, sems.at[b]))
            for c in copies:
                c.start()

            for c in copies:
                c.wait()

        half = n_t // 2
        for ref, slot, here in (
            (left_ref, t - half, t >= half),
            (right_ref, t + half, t < half),
            (last_ref, 0, t == n_t - 1),
            (first_ref, n_t - 1, t == 0),
        ):
            pl.when(here)(functools.partial(place, ref, slot))

    return pl.pallas_call(
        kernel,
        in_specs=[hbm if aligned else VMEM]
        + [VMEM] * 4
        + [pl.BlockSpec(memory_space=pl.ANY)] * len(after),
        out_specs=hbm if aligned else VMEM,
        out_shape=struct(payload.shape),
        input_output_aliases={0: 0} if aligned else {},
        scratch_shapes=[pltpu.SemaphoreType.DMA((per,))],
        compiler_params=params(60),
        cost_estimate=cost(0, 1024),
        name="place_last",
    )(payload, from_left, from_right, *ends, *after)


def gate_and_up(slices, gate, up, n_t, after):
    count, width, hb = slices[0].shape[0], gate.shape[0] // n_t, gate.shape[1]
    n_s = len(slices)

    def kernel(*refs):
        xs, gate_ref, up_ref = refs[:n_s], refs[n_s], refs[n_s + 1]
        pre_ref, w_ref, sems = refs[-3:]
        t = lax.axis_index("tensor")
        slots = [t, (t + n_t - 1) % n_t, (t + 1) % n_t, (t + n_t // 2) % n_t]
        copies = weight_copies(gate_ref, up_ref, w_ref, sems, slots, width)
        for c in copies:
            c.start()
        left = jnp.where(t == 0, xs[6][:, :width], xs[1][:, :width])
        right = jnp.where(t == n_t - 1, xs[5][:, :width], xs[2][:, :width])
        away = jnp.where(t < n_t // 2, xs[4][:, :width], xs[3][:, :width])
        pre = jnp.zeros((count, 2 * hb), jnp.float32)
        for i, x in enumerate([xs[0][:, :width], left, right, away]):
            copies[2 * i].wait()
            copies[2 * i + 1].wait()
            pre += jnp.dot(x, w_ref[i], preferred_element_type=jnp.float32)
        pre_ref[...] = pre

    return pl.pallas_call(
        kernel,
        in_specs=[VMEM] * n_s
        + [pl.BlockSpec(memory_space=pltpu.HBM)] * 2
        + [pl.BlockSpec(memory_space=pl.ANY)] * len(after),
        out_specs=VMEM,
        out_shape=struct((count, 2 * hb), jnp.float32),
        scratch_shapes=[
            pltpu.VMEM((n_t, width, 2 * hb), jnp.bfloat16),
            pltpu.SemaphoreType.DMA((2 * n_t,)),
        ],
        compiler_params=params(60),
        cost_estimate=cost(0, 1024),
        name="gate_and_up",
    )(*slices, gate, up, *after)


def gradients(pre, acts, slices, width):
    count, hb = pre.shape[0], pre.shape[1] // 2

    def kernel(pre_ref, *refs):
        act_refs, xs, out_ref = refs[: len(acts)], refs[len(acts) : -1], refs[-1]
        act = act_refs[0][...]
        for ref in act_refs[1:]:
            act += ref[...]
        act = act.T
        gate_pre, up_pre = pre_ref[:, :hb], pre_ref[:, hb:]
        s = jax.nn.sigmoid(gate_pre)
        gate_grad = act * up_pre * s * (1.0 + gate_pre * (1.0 - s))
        up_grad = act * gate_pre * s
        out_ref[:, :hb] = gate_grad.astype(jnp.bfloat16)
        out_ref[:, hb : 2 * hb] = up_grad.astype(jnp.bfloat16)
        for i, ref in enumerate(xs):

            @pl.when(lax.axis_index("tensor") == i)
            def _(ref=ref):
                out_ref[:, 2 * hb :] = ref[...]

    bucket = pl.BlockSpec((count, PB), lambda i: (0, width // PB))

    def whole(x):
        return pl.BlockSpec(x.shape, lambda i: (0, 0))

    return pl.pallas_call(
        kernel,
        grid=(1,),
        in_specs=[whole(x) for x in (pre, *acts)] + [bucket] * len(slices),
        out_specs=pl.BlockSpec((count, 2 * hb + PB), lambda i: (0, 0)),
        out_shape=struct((count, 2 * hb + PB)),
        compiler_params=params(60),
        cost_estimate=cost(0, 1024),
        name="gradients",
    )(pre, *acts, *slices)


def hand_over(teach, tok):
    n_dp, _, wide = teach.shape
    groups = n_dp // GROUP
    span = GROUP * tok
    digits = []
    if wide < tok:
        digits = teach[:, tok:].reshape(n_dp, 2, tok)
        digits = [jnp.pad(digits, ((0, 0), (0, 14), (0, 0)))]

    def kernel(*refs):
        teach_ref, (out_ref, total_ref) = refs[0], refs[-2:]

        def receivers(h, carry):
            total_ref[...] = jnp.zeros_like(total_ref)

            def sender(g, carry):
                lines = refs[1][g] if digits else teach_ref[g, tok : tok + 16, :tok]
                lines = lines.astype(jnp.float32)
                number = (lines[0:1] * float(LANES) + lines[1:2]).astype(jnp.int32)
                token = lax.broadcasted_iota(jnp.int32, (span, tok), 0) + h * span
                picks = (token == number).astype(jnp.float32).astype(jnp.bfloat16)
                total_ref[...] += jnp.dot(
                    picks, teach_ref[g, :tok], preferred_element_type=jnp.float32
                )
                return carry

            lax.fori_loop(0, n_dp, sender, 0)
            out_ref[pl.ds(h * GROUP, GROUP)] = (
                total_ref[...].astype(jnp.bfloat16).reshape(GROUP, tok, wide)
            )
            return carry

        lax.fori_loop(0, groups, receivers, 0)

    return pl.pallas_call(
        kernel,
        in_specs=[VMEM] * (1 + len(digits)),
        out_specs=VMEM,
        out_shape=struct((n_dp, tok, wide)),
        scratch_shapes=[pltpu.VMEM((span, wide), jnp.float32)],
        compiler_params=params(60),
        cost_estimate=cost(0, 1024),
        name="hand_over",
    )(teach, *digits)


def final_product(feats, handed, grads, masks):
    n_dp, count, cols = feats.shape
    wide = handed.shape[2]
    hb = (grads[0].shape[-1] - PB) // 2

    def kernel(feats_ref, handed_ref, *refs):
        grad_refs, (proj_ref, gate_ref, up_ref) = refs[: len(grads)], refs[len(grads) : len(grads) + 3]

        def group(g, totals):
            here = pl.ds(g * GROUP, GROUP)
            left = left_ref[here].reshape(GROUP * count, 2 * hb + PB)
            right = feats_ref[here].reshape(GROUP * count, cols)
            rows = handed_ref[here].reshape(GROUP * count, wide)
            return (
                totals[0] + contract_rows(left[:, : 2 * hb], right),
                totals[1] + contract_rows(left[:, 2 * hb :], rows),
            )

        totals = (jnp.zeros((2 * hb, cols), jnp.float32), jnp.zeros((PB, wide), jnp.float32))
        if masks:
            left_ref = refs[-1]
            for mask, ref in zip(masks, grad_refs):
                left_ref[lax.axis_index("dp") ^ mask] = ref[:count]
                left_ref[lax.axis_index("dp") ^ mask ^ 1] = ref[count:]
            totals = group(0, totals)
        else:
            left_ref = grad_refs[0]
            totals = lax.fori_loop(0, n_dp // GROUP, group, totals)
        gate_ref[...] = totals[0][:hb]
        up_ref[...] = totals[0][hb:]
        proj_ref[...] = totals[1].reshape(PB, 1, wide)

    return pl.pallas_call(
        kernel,
        in_specs=[VMEM] * (2 + len(grads)),
        out_specs=[VMEM] * 3,
        out_shape=[struct((PB, 1, wide), jnp.float32)] + [struct((hb, cols), jnp.float32)] * 2,
        scratch_shapes=[pltpu.VMEM((n_dp, count, 2 * hb + PB), jnp.bfloat16)] if masks else [],
        compiler_params=params(40),
        cost_estimate=cost(0, 1024),
        name="final_product",
    )(feats, handed, *grads)


def body(
    teacher_rows, row_map, student_hidden, projected, mlp_input, gate_bucket, up_bucket, down_bucket
):
    tok = row_map.shape[0]
    n_dp = lax.axis_size("dp")
    n_t = lax.axis_size("tensor")
    hb, width = down_bucket.shape[0], student_hidden.shape[1]
    cols = width * n_t // n_dp
    factor = 1.0 / math.sqrt(tok * n_dp)
    rows = hb // GROUP

    own, *pieces, teach = prepare(
        row_map, teacher_rows, mlp_input, student_hidden, projected, down_bucket, n_dp, n_t, factor
    )
    rightward = [(i, i + 1) for i in range(n_t - 1)]
    leftward = [(i + 1, i) for i in range(n_t - 1)]
    teach = lax.all_to_all(teach, "dp", split_axis=0, concat_axis=0, tiled=True)
    from_left, from_right = hop(own, rightward), hop(own, leftward)
    mine = stack_rows(
        [pieces[0]] + [shift(pieces[k], n_t, k) for k in range(1, n_t)], rows, width, 8
    )
    others = [swap(mine, n_dp, mask) for mask in (2, 4, 6)]

    from_left, from_right = ordered(from_left, mine), ordered(from_right, mine)
    far_left, far_right = hop(from_left, rightward[1:]), hop(from_right, leftward[:-1])
    ends = [hop(far_left, rightward[-1:]), hop(far_right, leftward[:1])]

    handed = hand_over(teach, tok)
    near = stack_rows(
        [mine] + others, n_t * rows, width, 60, after=[handed, far_left, far_right]
    )
    far = swap(near, n_dp, 1)
    partial = partial_products(near, far, student_hidden, projected, n_t, rows, factor, after=[])
    acts = [partial[0]] + [shift(partial[k], n_t, -k) for k in range(1, n_t)]

    sent = place_slices([own, from_left, from_right], [0, 1, n_t - 1], width, n_t, n_dp)
    sent = place_last(sent, far_left, far_right, ends, width, n_t, after=[partial[0]])
    feats = lax.all_to_all(sent, "dp", split_axis=0, concat_axis=0, tiled=True)

    slices = [own, from_left, from_right, far_left, far_right, *ends]
    pre = gate_and_up(slices, gate_bucket, up_bucket, n_t, after=[sent])
    grads = gradients(pre, acts, [own, from_left, far_left, ends[0]], width)
    masks = [0, 2, 4, 6] if n_dp == GROUP else []
    if masks:
        pair = stack_rows([grads, swap(grads, n_dp, 1)], tok, grads.shape[1], 8)
        grads = [pair] + [swap(pair, n_dp, mask) for mask in masks[1:]]
    else:
        grads = [lax.all_gather(grads, "dp")]
    return final_product(feats, handed, grads, masks)


def solution(mesh):
    in_specs = (
        P("dp", "tensor"),
        P("dp"),
        P("dp", "tensor"),
        P("dp", "tensor"),
        P("dp", "tensor"),
        P(None, "tensor"),
        P(None, "tensor"),
        P("tensor", None),
    )
    out_specs = (P(None, "tensor", "dp"), P("tensor", "dp"), P("tensor", "dp"))
    return jax.shard_map(body, mesh=mesh, in_specs=in_specs, out_specs=out_specs, check_vma=False)
```

```python
import functools
import math

import jax
import jax.numpy as jnp
from jax import lax
from jax.experimental import pallas as pl
from jax.experimental.pallas import tpu as pltpu
from jax.sharding import PartitionSpec as P

PB = 128
LANES = 128
GROUP = 8
MIB = 1 << 20

VMEM = pl.BlockSpec(memory_space=pltpu.VMEM)


def params(mib):
    return pltpu.CompilerParams(vmem_limit_bytes=mib * MIB)


def cost(flops, nbytes):
    return pl.CostEstimate(flops=int(flops), bytes_accessed=int(nbytes), transcendentals=0)


def struct(shape, dtype=jnp.bfloat16):
    return jax.ShapeDtypeStruct(shape, dtype)


def shift(x, count, by):
    return lax.ppermute(x, "tensor", [(i, (i + by) % count) for i in range(count)])


def hop(x, pairs):
    return lax.ppermute(x, "tensor", pairs)


def swap(x, count, mask):
    return lax.ppermute(x, "dp", [(i, i ^ mask) for i in range(count)])


def contract_rows(left, right):
    return lax.dot_general(
        left, right, (((0,), (0,)), ((), ())), preferred_element_type=jnp.float32
    )


def contract_cols(left, right):
    return lax.dot_general(
        left, right, (((1,), (1,)), ((), ())), preferred_element_type=jnp.float32
    )


def scaled_difference(student, projected, factor):
    wide = student.astype(jnp.float32) - projected.astype(jnp.float32)
    return (wide * factor).astype(jnp.bfloat16)


def prepare(row_map, teacher, mlp_input, student, projected, down, n_dp, n_t, factor):
    tok, width = mlp_input.shape
    rows = down.shape[0] // GROUP
    wide = teacher.shape[1] // n_dp
    hbm = pl.BlockSpec(memory_space=pltpu.HBM)
    if wide % LANES:
        blocks = teacher.reshape(tok, n_dp, wide).transpose(1, 0, 2)
        numbers = jnp.stack([row_map // LANES, row_map % LANES]).astype(jnp.bfloat16)
        numbers = jnp.broadcast_to(numbers.reshape(1, -1, wide), (n_dp, 2 * tok // wide, wide))
        blocks = jnp.concatenate([blocks, numbers], axis=1)
        wide = 0

    def kernel(m_ref, t_ref, x_ref, s_ref, p_ref, d_ref, own_ref, *refs):
        pieces, outs = refs[:n_t], refs[n_t:-4]
        s_buf, p_buf, m_buf, sems = refs[-4:]
        row = pl.multiple_of((lax.axis_index("dp") % GROUP) * rows, rows)
        pairs = [
            (s_ref.at[:, :PB], s_buf),
            (p_ref.at[:, :PB], p_buf),
            (m_ref, m_buf),
            (x_ref, own_ref.at[:, :width]),
        ]
        for k in range(n_t):
            col = pl.multiple_of(((lax.axis_index("tensor") + k) % n_t) * width, width)
            pairs.append((d_ref.at[pl.ds(row, rows), pl.ds(col, width)], pieces[k]))
        if wide:
            for i in range(n_dp):
                pairs.append((t_ref.at[:, i * wide : (i + 1) * wide], outs[0].at[i, :tok]))
        copies = [
            pltpu.make_async_copy(src, dst, sems.at[i]) for i, (src, dst) in enumerate(pairs)
        ]
        for c in copies:
            c.start()
        for c in copies[:3]:
            c.wait()
        own_ref[:, width:] = scaled_difference(s_buf[...], p_buf[...], factor)
        line = lax.broadcasted_iota(jnp.int32, (16, tok), 0)
        number = jnp.broadcast_to(m_buf[...], (16, tok))
        high, low = number // LANES, number % LANES
        digits = jnp.where(line == 0, high, jnp.where(line == 1, low, 0))
        digits = digits.astype(jnp.float32).astype(jnp.bfloat16)
        if wide:
            for i in range(n_dp):
                outs[0][i, tok:, :] = jnp.zeros((16, wide), jnp.bfloat16)
                outs[0][i, tok:, :tok] = digits
        for c in copies[3:]:
            c.wait()

    shapes = [(tok, width + PB)] + [(rows, width)] * n_t
    if wide:
        shapes.append((n_dp, tok + 16, wide))
    out = pl.pallas_call(
        kernel,
        in_specs=[hbm] * 6,
        out_specs=[VMEM] * len(shapes),
        out_shape=[struct(s) for s in shapes],
        scratch_shapes=[
            pltpu.VMEM((tok, PB), jnp.bfloat16),
            pltpu.VMEM((tok, PB), jnp.bfloat16),
            pltpu.VMEM((1, tok), jnp.int32),
            pltpu.SemaphoreType.DMA((4 + n_t + n_dp,)),
        ],
        compiler_params=params(60),
        cost_estimate=cost(0, 1024),
        name="prepare",
    )(row_map.reshape(1, tok), teacher, mlp_input, student, projected, down)
    return out if wide else [*out, blocks]


def stack_rows(parts, rows, width, mib, after=()):
    def kernel(*refs):
        out_ref = refs[-1]
        for i, ref in enumerate(refs[: len(parts)]):
            out_ref[i * rows : (i + 1) * rows] = ref[ref.shape[0] - rows :, :width]

    return pl.pallas_call(
        kernel,
        in_specs=[VMEM] * len(parts) + [pl.BlockSpec(memory_space=pl.ANY)] * len(after),
        out_specs=VMEM,
        out_shape=struct((len(parts) * rows, width)),
        compiler_params=params(mib),
        cost_estimate=cost(0, 1024),
        name="stack_rows",
    )(*parts, *after)


def ordered(x, *after):
    def kernel(*refs):
        pass

    return pl.pallas_call(
        kernel,
        in_specs=[pl.BlockSpec(memory_space=pl.ANY)] * (1 + len(after)),
        out_specs=pl.BlockSpec(memory_space=pl.ANY),
        out_shape=struct(x.shape, x.dtype),
        input_output_aliases={0: 0},
        compiler_params=params(1),
        cost_estimate=cost(0, 1024),
        name="ordered",
    )(x, *after)


def partial_products(near, far, student, projected, n_t, rows, factor, after):
    tok, width = student.shape
    hb = rows * GROUP
    half = GROUP // 2

    def kernel(near_ref, far_ref, s_ref, p_ref, *refs):
        outs = refs[len(after) :]
        err = scaled_difference(s_ref[...], p_ref[...], factor)
        place = lax.axis_index("dp") % GROUP
        for side, ref in enumerate((near_ref, far_ref)):
            product = contract_cols(ref[...], err)
            for j in range(half):
                row = pl.multiple_of((place ^ (2 * j + side)) * rows, rows)
                for k in range(n_t):
                    at = (j * n_t + k) * rows
                    outs[k][pl.ds(row, rows), :] = product[at : at + rows]

    return pl.pallas_call(
        kernel,
        in_specs=[VMEM] * 4
        + [pl.BlockSpec(memory_space=pl.ANY)] * len(after),
        out_specs=[VMEM] * n_t,
        out_shape=[struct((hb, tok), jnp.float32)] * n_t,
        compiler_params=params(60),
        cost_estimate=cost(0, 1024),
        name="partial_products",
    )(near, far, student, projected, *after)


def weight_copies(gate_ref, up_ref, w_ref, sems, slots, width):
    hb = gate_ref.shape[1]
    copies = []
    for i, slot in enumerate(slots):
        at = pl.ds(pl.multiple_of(slot * width, width), width)
        for j, ref in enumerate((gate_ref, up_ref)):
            dst = w_ref.at[i, :, j * hb : (j + 1) * hb]
            copies.append(pltpu.make_async_copy(ref.at[at], dst, sems.at[2 * i + j]))
    return copies


def place_slices(slices, places, width, n_t, n_dp):
    count = slices[0].shape[0]
    cols = width * n_t // n_dp
    per = width // cols

    def kernel(*refs):
        out_ref = refs[-1]
        for k, x_ref in zip(places, refs):
            slot = (lax.axis_index("tensor") + n_t - k) % n_t
            for b in range(per):
                out_ref[slot * per + b] = x_ref[:, b * cols : (b + 1) * cols]

    return pl.pallas_call(
        kernel,
        in_specs=[VMEM] * len(slices),
        out_specs=VMEM,
        out_shape=struct((n_dp, count, cols)),
        compiler_params=params(60),
        cost_estimate=cost(0, 1024),
        name="place_slices",
    )(*slices)


def place_last(payload, from_left, from_right, ends, width, n_t, after=()):
    n_dp = payload.shape[0]
    cols = width * n_t // n_dp
    per = width // cols
    aligned = cols % LANES == 0
    hbm = pl.BlockSpec(memory_space=pltpu.HBM)

    def kernel(in_ref, left_ref, right_ref, last_ref, first_ref, *refs):
        out_ref, sems = refs[len(after) :]
        t = lax.axis_index("tensor")
        if not aligned:
            out_ref[...] = in_ref[...]

        def place(ref, slot):
            if not aligned:
                for b in range(per):
                    out_ref[slot * per + b] = ref[:, b * cols : (b + 1) * cols]
                return
            copies = []
            for b in range(per):
                src = ref.at[:, pl.ds(b * cols, cols)]
                dst = out_ref.at[slot * per + b]
                copies.append(pltpu.make_async_copy(src, dst, sems.at[b]))
            for c in copies:
                c.start()

            for c in copies:
                c.wait()

        half = n_t // 2
        for ref, slot, here in (
            (left_ref, t - half, t >= half),
            (right_ref, t + half, t < half),
            (last_ref, 0, t == n_t - 1),
            (first_ref, n_t - 1, t == 0),
        ):
            pl.when(here)(functools.partial(place, ref, slot))

    return pl.pallas_call(
        kernel,
        in_specs=[hbm if aligned else VMEM]
        + [VMEM] * 4
        + [pl.BlockSpec(memory_space=pl.ANY)] * len(after),
        out_specs=hbm if aligned else VMEM,
        out_shape=struct(payload.shape),
        input_output_aliases={0: 0} if aligned else {},
        scratch_shapes=[pltpu.SemaphoreType.DMA((per,))],
        compiler_params=params(60),
        cost_estimate=cost(0, 1024),
        name="place_last",
    )(payload, from_left, from_right, *ends, *after)


def gate_and_up(slices, gate, up, n_t, after):
    count, width, hb = slices[0].shape[0], gate.shape[0] // n_t, gate.shape[1]
    n_s = len(slices)

    def kernel(*refs):
        xs, gate_ref, up_ref = refs[:n_s], refs[n_s], refs[n_s + 1]
        pre_ref, w_ref, sems = refs[-3:]
        t = lax.axis_index("tensor")
        slots = [t, (t + n_t - 1) % n_t, (t + 1) % n_t, (t + n_t // 2) % n_t]
        copies = weight_copies(gate_ref, up_ref, w_ref, sems, slots, width)
        for c in copies:
            c.start()
        left = jnp.where(t == 0, xs[6][:, :width], xs[1][:, :width])
        right = jnp.where(t == n_t - 1, xs[5][:, :width], xs[2][:, :width])
        away = jnp.where(t < n_t // 2, xs[4][:, :width], xs[3][:, :width])
        pre = jnp.zeros((count, 2 * hb), jnp.float32)
        for i, x in enumerate([xs[0][:, :width], left, right, away]):
            copies[2 * i].wait()
            copies[2 * i + 1].wait()
            pre += jnp.dot(x, w_ref[i], preferred_element_type=jnp.float32)
        pre_ref[...] = pre

    return pl.pallas_call(
        kernel,
        in_specs=[VMEM] * n_s
        + [pl.BlockSpec(memory_space=pltpu.HBM)] * 2
        + [pl.BlockSpec(memory_space=pl.ANY)] * len(after),
        out_specs=VMEM,
        out_shape=struct((count, 2 * hb), jnp.float32),
        scratch_shapes=[
            pltpu.VMEM((n_t, width, 2 * hb), jnp.bfloat16),
            pltpu.SemaphoreType.DMA((2 * n_t,)),
        ],
        compiler_params=params(60),
        cost_estimate=cost(0, 1024),
        name="gate_and_up",
    )(*slices, gate, up, *after)


def gradients(pre, acts, slices, width):
    count, hb = pre.shape[0], pre.shape[1] // 2

    def kernel(pre_ref, *refs):
        act_refs, xs, out_ref = refs[: len(acts)], refs[len(acts) : -1], refs[-1]
        act = act_refs[0][...]
        for ref in act_refs[1:]:
            act += ref[...]
        act = act.T
        gate_pre, up_pre = pre_ref[:, :hb], pre_ref[:, hb:]
        s = jax.nn.sigmoid(gate_pre)
        gate_grad = act * up_pre * s * (1.0 + gate_pre * (1.0 - s))
        up_grad = act * gate_pre * s
        out_ref[:, :hb] = gate_grad.astype(jnp.bfloat16)
        out_ref[:, hb : 2 * hb] = up_grad.astype(jnp.bfloat16)
        for i, ref in enumerate(xs):

            @pl.when(lax.axis_index("tensor") == i)
            def _(ref=ref):
                out_ref[:, 2 * hb :] = ref[...]

    bucket = pl.BlockSpec((count, PB), lambda i: (0, width // PB))

    def whole(x):
        return pl.BlockSpec(x.shape, lambda i: (0, 0))

    return pl.pallas_call(
        kernel,
        grid=(1,),
        in_specs=[whole(x) for x in (pre, *acts)] + [bucket] * len(slices),
        out_specs=pl.BlockSpec((count, 2 * hb + PB), lambda i: (0, 0)),
        out_shape=struct((count, 2 * hb + PB)),
        compiler_params=params(60),
        cost_estimate=cost(0, 1024),
        name="gradients",
    )(pre, *acts, *slices)


def hand_over(teach, tok):
    n_dp, _, wide = teach.shape
    groups = n_dp // GROUP
    span = GROUP * tok
    digits = []
    if wide < tok:
        digits = teach[:, tok:].reshape(n_dp, 2, tok)
        digits = [jnp.pad(digits, ((0, 0), (0, 14), (0, 0)))]

    def kernel(*refs):
        teach_ref, (out_ref, total_ref) = refs[0], refs[-2:]

        def receivers(h, carry):
            total_ref[...] = jnp.zeros_like(total_ref)

            def sender(g, carry):
                lines = refs[1][g] if digits else teach_ref[g, tok : tok + 16, :tok]
                lines = lines.astype(jnp.float32)
                number = (lines[0:1] * float(LANES) + lines[1:2]).astype(jnp.int32)
                token = lax.broadcasted_iota(jnp.int32, (span, tok), 0) + h * span
                picks = (token == number).astype(jnp.float32).astype(jnp.bfloat16)
                total_ref[...] += jnp.dot(
                    picks, teach_ref[g, :tok], preferred_element_type=jnp.float32
                )
                return carry

            lax.fori_loop(0, n_dp, sender, 0)
            out_ref[pl.ds(h * GROUP, GROUP)] = (
                total_ref[...].astype(jnp.bfloat16).reshape(GROUP, tok, wide)
            )
            return carry

        lax.fori_loop(0, groups, receivers, 0)

    return pl.pallas_call(
        kernel,
        in_specs=[VMEM] * (1 + len(digits)),
        out_specs=VMEM,
        out_shape=struct((n_dp, tok, wide)),
        scratch_shapes=[pltpu.VMEM((span, wide), jnp.float32)],
        compiler_params=params(60),
        cost_estimate=cost(0, 1024),
        name="hand_over",
    )(teach, *digits)


def final_product(feats, handed, grads, masks):
    n_dp, count, cols = feats.shape
    wide = handed.shape[2]
    hb = (grads[0].shape[-1] - PB) // 2

    def kernel(feats_ref, handed_ref, *refs):
        grad_refs, (proj_ref, gate_ref, up_ref) = refs[: len(grads)], refs[len(grads) : len(grads) + 3]

        def group(g, totals):
            here = pl.ds(g * GROUP, GROUP)
            left = left_ref[here].reshape(GROUP * count, 2 * hb + PB)
            right = feats_ref[here].reshape(GROUP * count, cols)
            rows = handed_ref[here].reshape(GROUP * count, wide)
            return (
                totals[0] + contract_rows(left[:, : 2 * hb], right),
                totals[1] + contract_rows(left[:, 2 * hb :], rows),
            )

        totals = (jnp.zeros((2 * hb, cols), jnp.float32), jnp.zeros((PB, wide), jnp.float32))
        if masks:
            left_ref = refs[-1]
            for mask, ref in zip(masks, grad_refs):
                for j in range(GROUP // 2):
                    place = lax.axis_index("dp") ^ mask ^ (2 * j)
                    left_ref[place] = ref[j * count : (j + 1) * count]
            totals = group(0, totals)
        else:
            left_ref = grad_refs[0]
            totals = lax.fori_loop(0, n_dp // GROUP, group, totals)
        gate_ref[...] = totals[0][:hb]
        up_ref[...] = totals[0][hb:]
        proj_ref[...] = totals[1].reshape(PB, 1, wide)

    return pl.pallas_call(
        kernel,
        in_specs=[VMEM] * (2 + len(grads)),
        out_specs=[VMEM] * 3,
        out_shape=[struct((PB, 1, wide), jnp.float32)] + [struct((hb, cols), jnp.float32)] * 2,
        scratch_shapes=[pltpu.VMEM((n_dp, count, 2 * hb + PB), jnp.bfloat16)] if masks else [],
        compiler_params=params(60),
        cost_estimate=cost(0, 1024),
        name="final_product",
    )(feats, handed, *grads)


def body(
    teacher_rows, row_map, student_hidden, projected, mlp_input, gate_bucket, up_bucket, down_bucket
):
    tok = row_map.shape[0]
    n_dp = lax.axis_size("dp")
    n_t = lax.axis_size("tensor")
    hb, width = down_bucket.shape[0], student_hidden.shape[1]
    cols = width * n_t // n_dp
    factor = 1.0 / math.sqrt(tok * n_dp)
    rows = hb // GROUP

    own, *pieces, teach = prepare(
        row_map, teacher_rows, mlp_input, student_hidden, projected, down_bucket, n_dp, n_t, factor
    )
    rightward = [(i, i + 1) for i in range(n_t - 1)]
    leftward = [(i + 1, i) for i in range(n_t - 1)]
    teach = lax.all_to_all(teach, "dp", split_axis=0, concat_axis=0, tiled=True)
    mine = stack_rows(
        [pieces[0]] + [shift(pieces[k], n_t, k) for k in range(1, n_t)], rows, width, 8
    )
    others = [swap(mine, n_dp, mask) for mask in (2, 4, 6)]

    own = ordered(own, mine)
    from_left, from_right = hop(own, rightward), hop(own, leftward)
    far_left, far_right = hop(from_left, rightward[1:]), hop(from_right, leftward[:-1])
    ends = [hop(far_left, rightward[-1:]), hop(far_right, leftward[:1])]

    handed = hand_over(teach, tok)
    near = stack_rows([mine] + others, n_t * rows, width, 60)
    far = swap(near, n_dp, 1)
    partial = partial_products(near, far, student_hidden, projected, n_t, rows, factor, after=[])
    acts = [partial[0]] + [shift(partial[k], n_t, -k) for k in range(1, n_t)]

    sent = place_slices([own, from_left, from_right], [0, 1, n_t - 1], width, n_t, n_dp)
    sent = place_last(sent, far_left, far_right, ends, width, n_t, after=[partial[0], handed])
    feats = lax.all_to_all(sent, "dp", split_axis=0, concat_axis=0, tiled=True)

    slices = [own, from_left, from_right, far_left, far_right, *ends]
    pre = gate_and_up(slices, gate_bucket, up_bucket, n_t, after=[sent])
    grads = gradients(pre, acts, [own, from_left, far_left, ends[0]], width)
    masks = [0, 1] if n_dp == GROUP else []
    if masks:
        near = [grads] + [swap(grads, n_dp, mask) for mask in (2, 4, 6)]
        near = stack_rows(near, tok, grads.shape[1], 8)
        grads = [near, swap(near, n_dp, 1)]
    else:
        grads = [lax.all_gather(grads, "dp")]
    return final_product(feats, handed, grads, masks)


def solution(mesh):
    in_specs = (
        P("dp", "tensor"),
        P("dp"),
        P("dp", "tensor"),
        P("dp", "tensor"),
        P("dp", "tensor"),
        P(None, "tensor"),
        P(None, "tensor"),
        P("tensor", None),
    )
    out_specs = (P(None, "tensor", "dp"), P("tensor", "dp"), P("tensor", "dp"))
    return jax.shard_map(body, mesh=mesh, in_specs=in_specs, out_specs=out_specs, check_vma=False)
```

```python
import functools
import math

import jax
import jax.numpy as jnp
from jax import lax
from jax.experimental import pallas as pl
from jax.experimental.pallas import tpu as pltpu
from jax.sharding import PartitionSpec as P

PB = 128
LANES = 128
GROUP = 8
MIB = 1 << 20

VMEM = pl.BlockSpec(memory_space=pltpu.VMEM)


def params(mib):
    return pltpu.CompilerParams(vmem_limit_bytes=mib * MIB)


def cost(flops, nbytes):
    return pl.CostEstimate(flops=int(flops), bytes_accessed=int(nbytes), transcendentals=0)


def struct(shape, dtype=jnp.bfloat16):
    return jax.ShapeDtypeStruct(shape, dtype)


def shift(x, count, by):
    return lax.ppermute(x, "tensor", [(i, (i + by) % count) for i in range(count)])


def hop(x, pairs):
    return lax.ppermute(x, "tensor", pairs)


def swap(x, count, mask):
    return lax.ppermute(x, "dp", [(i, i ^ mask) for i in range(count)])


def contract_rows(left, right):
    return lax.dot_general(
        left, right, (((0,), (0,)), ((), ())), preferred_element_type=jnp.float32
    )


def contract_cols(left, right):
    return lax.dot_general(
        left, right, (((1,), (1,)), ((), ())), preferred_element_type=jnp.float32
    )


def scaled_difference(student, projected, factor):
    wide = student.astype(jnp.float32) - projected.astype(jnp.float32)
    return (wide * factor).astype(jnp.bfloat16)


def prepare(row_map, teacher, mlp_input, student, projected, down, n_dp, n_t, factor):
    tok, width = mlp_input.shape
    rows = down.shape[0] // GROUP
    wide = teacher.shape[1] // n_dp
    hbm = pl.BlockSpec(memory_space=pltpu.HBM)
    if wide % LANES:
        blocks = teacher.reshape(tok, n_dp, wide).transpose(1, 0, 2)
        numbers = jnp.stack([row_map // LANES, row_map % LANES]).astype(jnp.bfloat16)
        numbers = jnp.broadcast_to(numbers.reshape(1, -1, wide), (n_dp, 2 * tok // wide, wide))
        blocks = jnp.concatenate([blocks, numbers], axis=1)
        wide = 0

    def kernel(m_ref, t_ref, x_ref, s_ref, p_ref, d_ref, own_ref, *refs):
        pieces, outs = refs[:n_t], refs[n_t:-4]
        s_buf, p_buf, m_buf, sems = refs[-4:]
        row = pl.multiple_of((lax.axis_index("dp") % GROUP) * rows, rows)
        pairs = [
            (s_ref.at[:, :PB], s_buf),
            (p_ref.at[:, :PB], p_buf),
            (m_ref, m_buf),
            (x_ref, own_ref.at[:, :width]),
        ]
        for k in range(n_t):
            col = pl.multiple_of(((lax.axis_index("tensor") + k) % n_t) * width, width)
            pairs.append((d_ref.at[pl.ds(row, rows), pl.ds(col, width)], pieces[k]))
        if wide:
            for i in range(n_dp):
                pairs.append((t_ref.at[:, i * wide : (i + 1) * wide], outs[0].at[i, :tok]))
        copies = [
            pltpu.make_async_copy(src, dst, sems.at[i]) for i, (src, dst) in enumerate(pairs)
        ]
        for c in copies:
            c.start()
        for c in copies[:3]:
            c.wait()
        own_ref[:, width:] = scaled_difference(s_buf[...], p_buf[...], factor)
        line = lax.broadcasted_iota(jnp.int32, (16, tok), 0)
        number = jnp.broadcast_to(m_buf[...], (16, tok))
        high, low = number // LANES, number % LANES
        digits = jnp.where(line == 0, high, jnp.where(line == 1, low, 0))
        digits = digits.astype(jnp.float32).astype(jnp.bfloat16)
        if wide:
            for i in range(n_dp):
                outs[0][i, tok:, :] = jnp.zeros((16, wide), jnp.bfloat16)
                outs[0][i, tok:, :tok] = digits
        for c in copies[3:]:
            c.wait()

    shapes = [(tok, width + PB)] + [(rows, width)] * n_t
    if wide:
        shapes.append((n_dp, tok + 16, wide))
    out = pl.pallas_call(
        kernel,
        in_specs=[hbm] * 6,
        out_specs=[VMEM] * len(shapes),
        out_shape=[struct(s) for s in shapes],
        scratch_shapes=[
            pltpu.VMEM((tok, PB), jnp.bfloat16),
            pltpu.VMEM((tok, PB), jnp.bfloat16),
            pltpu.VMEM((1, tok), jnp.int32),
            pltpu.SemaphoreType.DMA((4 + n_t + n_dp,)),
        ],
        compiler_params=params(60),
        cost_estimate=cost(0, 1024),
        name="prepare",
    )(row_map.reshape(1, tok), teacher, mlp_input, student, projected, down)
    return out if wide else [*out, blocks]


def stack_rows(parts, rows, width, mib, after=()):
    def kernel(*refs):
        out_ref = refs[-1]
        for i, ref in enumerate(refs[: len(parts)]):
            out_ref[i * rows : (i + 1) * rows] = ref[ref.shape[0] - rows :, :width]

    return pl.pallas_call(
        kernel,
        in_specs=[VMEM] * len(parts) + [pl.BlockSpec(memory_space=pl.ANY)] * len(after),
        out_specs=VMEM,
        out_shape=struct((len(parts) * rows, width)),
        compiler_params=params(mib),
        cost_estimate=cost(0, 1024),
        name="stack_rows",
    )(*parts, *after)


def ordered(x, *after):
    def kernel(*refs):
        pass

    return pl.pallas_call(
        kernel,
        in_specs=[pl.BlockSpec(memory_space=pl.ANY)] * (1 + len(after)),
        out_specs=pl.BlockSpec(memory_space=pl.ANY),
        out_shape=struct(x.shape, x.dtype),
        input_output_aliases={0: 0},
        compiler_params=params(1),
        cost_estimate=cost(0, 1024),
        name="ordered",
    )(x, *after)


def partial_products(near, far, student, projected, n_t, rows, factor, after):
    tok, width = student.shape
    hb = rows * GROUP
    half = GROUP // 2

    def kernel(near_ref, far_ref, s_ref, p_ref, *refs):
        outs = refs[len(after) :]
        err = scaled_difference(s_ref[...], p_ref[...], factor)
        place = lax.axis_index("dp") % GROUP
        for side, ref in enumerate((near_ref, far_ref)):
            product = contract_cols(ref[...], err)
            for j in range(half):
                row = pl.multiple_of((place ^ (2 * j + side)) * rows, rows)
                for k in range(n_t):
                    at = (j * n_t + k) * rows
                    outs[k][pl.ds(row, rows), :] = product[at : at + rows]

    return pl.pallas_call(
        kernel,
        in_specs=[VMEM] * 4
        + [pl.BlockSpec(memory_space=pl.ANY)] * len(after),
        out_specs=[VMEM] * n_t,
        out_shape=[struct((hb, tok), jnp.float32)] * n_t,
        compiler_params=params(60),
        cost_estimate=cost(0, 1024),
        name="partial_products",
    )(near, far, student, projected, *after)


def weight_copies(gate_ref, up_ref, w_ref, sems, slots, width):
    hb = gate_ref.shape[1]
    copies = []
    for i, slot in enumerate(slots):
        at = pl.ds(pl.multiple_of(slot * width, width), width)
        for j, ref in enumerate((gate_ref, up_ref)):
            dst = w_ref.at[i, :, j * hb : (j + 1) * hb]
            copies.append(pltpu.make_async_copy(ref.at[at], dst, sems.at[2 * i + j]))
    return copies


def place_slices(slices, places, width, n_t, n_dp, after):
    count = slices[0].shape[0]
    cols = width * n_t // n_dp
    per = width // cols

    def kernel(*refs):
        out_ref = refs[-1]
        for k, x_ref in zip(places, refs):
            slot = (lax.axis_index("tensor") + n_t - k) % n_t
            for b in range(per):
                out_ref[slot * per + b] = x_ref[:, b * cols : (b + 1) * cols]

    return pl.pallas_call(
        kernel,
        in_specs=[VMEM] * len(slices) + [pl.BlockSpec(memory_space=pl.ANY)] * len(after),
        out_specs=VMEM,
        out_shape=struct((n_dp, count, cols)),
        compiler_params=params(60),
        cost_estimate=cost(0, 1024),
        name="place_slices",
    )(*slices, *after)


def place_last(payload, from_left, from_right, ends, width, n_t, after=()):
    n_dp = payload.shape[0]
    cols = width * n_t // n_dp
    per = width // cols
    aligned = cols % LANES == 0
    hbm = pl.BlockSpec(memory_space=pltpu.HBM)

    def kernel(in_ref, left_ref, right_ref, last_ref, first_ref, *refs):
        out_ref, sems = refs[len(after) :]
        t = lax.axis_index("tensor")
        if not aligned:
            out_ref[...] = in_ref[...]

        def place(ref, slot):
            if not aligned:
                for b in range(per):
                    out_ref[slot * per + b] = ref[:, b * cols : (b + 1) * cols]
                return
            copies = []
            for b in range(per):
                src = ref.at[:, pl.ds(b * cols, cols)]
                dst = out_ref.at[slot * per + b]
                copies.append(pltpu.make_async_copy(src, dst, sems.at[b]))
            for c in copies:
                c.start()

            for c in copies:
                c.wait()

        half = n_t // 2
        for ref, slot, here in (
            (left_ref, t - half, t >= half),
            (right_ref, t + half, t < half),
            (last_ref, 0, t == n_t - 1),
            (first_ref, n_t - 1, t == 0),
        ):
            pl.when(here)(functools.partial(place, ref, slot))

    return pl.pallas_call(
        kernel,
        in_specs=[hbm if aligned else VMEM]
        + [VMEM] * 4
        + [pl.BlockSpec(memory_space=pl.ANY)] * len(after),
        out_specs=hbm if aligned else VMEM,
        out_shape=struct(payload.shape),
        input_output_aliases={0: 0} if aligned else {},
        scratch_shapes=[pltpu.SemaphoreType.DMA((per,))],
        compiler_params=params(60),
        cost_estimate=cost(0, 1024),
        name="place_last",
    )(payload, from_left, from_right, *ends, *after)


def gate_and_up(slices, gate, up, n_t, after):
    count, width, hb = slices[0].shape[0], gate.shape[0] // n_t, gate.shape[1]
    n_s = len(slices)

    def kernel(*refs):
        xs, gate_ref, up_ref = refs[:n_s], refs[n_s], refs[n_s + 1]
        pre_ref, w_ref, sems = refs[-3:]
        t = lax.axis_index("tensor")
        slots = [t, (t + n_t - 1) % n_t, (t + 1) % n_t, (t + n_t // 2) % n_t]
        copies = weight_copies(gate_ref, up_ref, w_ref, sems, slots, width)
        for c in copies:
            c.start()
        left = jnp.where(t == 0, xs[6][:, :width], xs[1][:, :width])
        right = jnp.where(t == n_t - 1, xs[5][:, :width], xs[2][:, :width])
        away = jnp.where(t < n_t // 2, xs[4][:, :width], xs[3][:, :width])
        pre = jnp.zeros((count, 2 * hb), jnp.float32)
        for i, x in enumerate([xs[0][:, :width], left, right, away]):
            copies[2 * i].wait()
            copies[2 * i + 1].wait()
            pre += jnp.dot(x, w_ref[i], preferred_element_type=jnp.float32)
        pre_ref[...] = pre

    return pl.pallas_call(
        kernel,
        in_specs=[VMEM] * n_s
        + [pl.BlockSpec(memory_space=pltpu.HBM)] * 2
        + [pl.BlockSpec(memory_space=pl.ANY)] * len(after),
        out_specs=VMEM,
        out_shape=struct((count, 2 * hb), jnp.float32),
        scratch_shapes=[
            pltpu.VMEM((n_t, width, 2 * hb), jnp.bfloat16),
            pltpu.SemaphoreType.DMA((2 * n_t,)),
        ],
        compiler_params=params(60),
        cost_estimate=cost(0, 1024),
        name="gate_and_up",
    )(*slices, gate, up, *after)


def gradients(pre, acts, slices, width):
    count, hb = pre.shape[0], pre.shape[1] // 2

    def kernel(pre_ref, *refs):
        act_refs, xs, out_ref = refs[: len(acts)], refs[len(acts) : -1], refs[-1]
        act = act_refs[0][...]
        for ref in act_refs[1:]:
            act += ref[...]
        act = act.T
        gate_pre, up_pre = pre_ref[:, :hb], pre_ref[:, hb:]
        s = jax.nn.sigmoid(gate_pre)
        gate_grad = act * up_pre * s * (1.0 + gate_pre * (1.0 - s))
        up_grad = act * gate_pre * s
        out_ref[:, :hb] = gate_grad.astype(jnp.bfloat16)
        out_ref[:, hb : 2 * hb] = up_grad.astype(jnp.bfloat16)
        for i, ref in enumerate(xs):

            @pl.when(lax.axis_index("tensor") == i)
            def _(ref=ref):
                out_ref[:, 2 * hb :] = ref[...]

    bucket = pl.BlockSpec((count, PB), lambda i: (0, width // PB))

    def whole(x):
        return pl.BlockSpec(x.shape, lambda i: (0, 0))

    return pl.pallas_call(
        kernel,
        grid=(1,),
        in_specs=[whole(x) for x in (pre, *acts)] + [bucket] * len(slices),
        out_specs=pl.BlockSpec((count, 2 * hb + PB), lambda i: (0, 0)),
        out_shape=struct((count, 2 * hb + PB)),
        compiler_params=params(60),
        cost_estimate=cost(0, 1024),
        name="gradients",
    )(pre, *acts, *slices)


def hand_over(teach, tok):
    n_dp, _, wide = teach.shape
    groups = n_dp // GROUP
    span = GROUP * tok
    digits = []
    if wide < tok:
        digits = teach[:, tok:].reshape(n_dp, 2, tok)
        digits = [jnp.pad(digits, ((0, 0), (0, 14), (0, 0)))]

    def kernel(*refs):
        teach_ref, (out_ref, total_ref) = refs[0], refs[-2:]

        def receivers(h, carry):
            total_ref[...] = jnp.zeros_like(total_ref)

            def sender(g, carry):
                lines = refs[1][g] if digits else teach_ref[g, tok : tok + 16, :tok]
                lines = lines.astype(jnp.float32)
                number = (lines[0:1] * float(LANES) + lines[1:2]).astype(jnp.int32)
                token = lax.broadcasted_iota(jnp.int32, (span, tok), 0) + h * span
                picks = (token == number).astype(jnp.float32).astype(jnp.bfloat16)
                total_ref[...] += jnp.dot(
                    picks, teach_ref[g, :tok], preferred_element_type=jnp.float32
                )
                return carry

            lax.fori_loop(0, n_dp, sender, 0)
            out_ref[pl.ds(h * GROUP, GROUP)] = (
                total_ref[...].astype(jnp.bfloat16).reshape(GROUP, tok, wide)
            )
            return carry

        lax.fori_loop(0, groups, receivers, 0)

    return pl.pallas_call(
        kernel,
        in_specs=[VMEM] * (1 + len(digits)),
        out_specs=VMEM,
        out_shape=struct((n_dp, tok, wide)),
        scratch_shapes=[pltpu.VMEM((span, wide), jnp.float32)],
        compiler_params=params(60),
        cost_estimate=cost(0, 1024),
        name="hand_over",
    )(teach, *digits)


def final_product(feats, handed, grads, masks):
    n_dp, count, cols = feats.shape
    wide = handed.shape[2]
    hb = (grads[0].shape[-1] - PB) // 2

    def kernel(feats_ref, handed_ref, *refs):
        grad_refs, (proj_ref, gate_ref, up_ref) = refs[: len(grads)], refs[len(grads) : len(grads) + 3]

        def group(g, totals):
            here = pl.ds(g * GROUP, GROUP)
            left = left_ref[here].reshape(GROUP * count, 2 * hb + PB)
            right = feats_ref[here].reshape(GROUP * count, cols)
            rows = handed_ref[here].reshape(GROUP * count, wide)
            return (
                totals[0] + contract_rows(left[:, : 2 * hb], right),
                totals[1] + contract_rows(left[:, 2 * hb :], rows),
            )

        totals = (jnp.zeros((2 * hb, cols), jnp.float32), jnp.zeros((PB, wide), jnp.float32))
        if masks:
            left_ref = refs[-1]
            for mask, ref in zip(masks, grad_refs):
                left_ref[lax.axis_index("dp") ^ mask] = ref[:count]
                left_ref[lax.axis_index("dp") ^ mask ^ 1] = ref[count:]
            totals = group(0, totals)
        else:
            left_ref = grad_refs[0]
            totals = lax.fori_loop(0, n_dp // GROUP, group, totals)
        gate_ref[...] = totals[0][:hb]
        up_ref[...] = totals[0][hb:]
        proj_ref[...] = totals[1].reshape(PB, 1, wide)

    return pl.pallas_call(
        kernel,
        in_specs=[VMEM] * (2 + len(grads)),
        out_specs=[VMEM] * 3,
        out_shape=[struct((PB, 1, wide), jnp.float32)] + [struct((hb, cols), jnp.float32)] * 2,
        scratch_shapes=[pltpu.VMEM((n_dp, count, 2 * hb + PB), jnp.bfloat16)] if masks else [],
        compiler_params=params(40),
        cost_estimate=cost(0, 1024),
        name="final_product",
    )(feats, handed, *grads)


def body(
    teacher_rows, row_map, student_hidden, projected, mlp_input, gate_bucket, up_bucket, down_bucket
):
    tok = row_map.shape[0]
    n_dp = lax.axis_size("dp")
    n_t = lax.axis_size("tensor")
    hb, width = down_bucket.shape[0], student_hidden.shape[1]
    cols = width * n_t // n_dp
    factor = 1.0 / math.sqrt(tok * n_dp)
    rows = hb // GROUP

    own, *pieces, teach = prepare(
        row_map, teacher_rows, mlp_input, student_hidden, projected, down_bucket, n_dp, n_t, factor
    )
    rightward = [(i, i + 1) for i in range(n_t - 1)]
    leftward = [(i + 1, i) for i in range(n_t - 1)]
    teach = lax.all_to_all(teach, "dp", split_axis=0, concat_axis=0, tiled=True)
    mine = stack_rows(
        [pieces[0]] + [shift(pieces[k], n_t, k) for k in range(1, n_t)], rows, width, 8
    )
    others = [swap(mine, n_dp, mask) for mask in (2, 4, 6)]

    own = ordered(own, mine)
    from_left, from_right = hop(own, rightward), hop(own, leftward)
    far_left, far_right = hop(from_left, rightward[1:]), hop(from_right, leftward[:-1])
    ends = [hop(far_left, rightward[-1:]), hop(far_right, leftward[:1])]

    handed = hand_over(teach, tok)
    near = stack_rows([mine] + others, n_t * rows, width, 60)
    far = swap(near, n_dp, 1)
    partial = partial_products(near, far, student_hidden, projected, n_t, rows, factor, after=[])
    acts = [partial[0]] + [shift(partial[k], n_t, -k) for k in range(1, n_t)]

    sent = place_slices([own, from_left, from_right], [0, 1, n_t - 1], width, n_t, n_dp, [])
    sent = place_last(sent, far_left, far_right, ends, width, n_t, after=[partial[0], teach])
    feats = lax.all_to_all(sent, "dp", split_axis=0, concat_axis=0, tiled=True)

    slices = [own, from_left, from_right, far_left, far_right, *ends]
    pre = gate_and_up(slices, gate_bucket, up_bucket, n_t, after=[sent])
    grads = gradients(pre, acts, [own, from_left, far_left, ends[0]], width)
    masks = [0, 2, 4, 6] if n_dp == GROUP else []
    if masks:
        pair = stack_rows([grads, swap(grads, n_dp, 1)], tok, grads.shape[1], 8)
        grads = [pair] + [swap(pair, n_dp, mask) for mask in masks[1:]]
    else:
        grads = [lax.all_gather(grads, "dp")]
    return final_product(feats, handed, grads, masks)


def solution(mesh):
    in_specs = (
        P("dp", "tensor"),
        P("dp"),
        P("dp", "tensor"),
        P("dp", "tensor"),
        P("dp", "tensor"),
        P(None, "tensor"),
        P(None, "tensor"),
        P("tensor", None),
    )
    out_specs = (P(None, "tensor", "dp"), P("tensor", "dp"), P("tensor", "dp"))
    return jax.shard_map(body, mesh=mesh, in_specs=in_specs, out_specs=out_specs, check_vma=False)
```

```python
import functools
import math

import jax
import jax.numpy as jnp
from jax import lax
from jax.experimental import pallas as pl
from jax.experimental.pallas import tpu as pltpu
from jax.sharding import PartitionSpec as P

PB = 128
LANES = 128
GROUP = 8
MIB = 1 << 20

VMEM = pl.BlockSpec(memory_space=pltpu.VMEM)


def params(mib):
    return pltpu.CompilerParams(vmem_limit_bytes=mib * MIB)


def cost(flops, nbytes):
    return pl.CostEstimate(flops=int(flops), bytes_accessed=int(nbytes), transcendentals=0)


def struct(shape, dtype=jnp.bfloat16):
    return jax.ShapeDtypeStruct(shape, dtype)


def shift(x, count, by):
    return lax.ppermute(x, "tensor", [(i, (i + by) % count) for i in range(count)])


def hop(x, pairs):
    return lax.ppermute(x, "tensor", pairs)


def swap(x, count, mask):
    return lax.ppermute(x, "dp", [(i, i ^ mask) for i in range(count)])


def contract_rows(left, right):
    return lax.dot_general(
        left, right, (((0,), (0,)), ((), ())), preferred_element_type=jnp.float32
    )


def contract_cols(left, right):
    return lax.dot_general(
        left, right, (((1,), (1,)), ((), ())), preferred_element_type=jnp.float32
    )


def scaled_difference(student, projected, factor):
    wide = student.astype(jnp.float32) - projected.astype(jnp.float32)
    return (wide * factor).astype(jnp.bfloat16)


def prepare(row_map, teacher, mlp_input, student, projected, down, n_dp, n_t, factor):
    tok, width = mlp_input.shape
    rows = down.shape[0] // GROUP
    wide = teacher.shape[1] // n_dp
    hbm = pl.BlockSpec(memory_space=pltpu.HBM)
    if wide % LANES:
        blocks = teacher.reshape(tok, n_dp, wide).transpose(1, 0, 2)
        numbers = jnp.stack([row_map // LANES, row_map % LANES]).astype(jnp.bfloat16)
        numbers = jnp.broadcast_to(numbers.reshape(1, -1, wide), (n_dp, 2 * tok // wide, wide))
        blocks = jnp.concatenate([blocks, numbers], axis=1)
        wide = 0

    def kernel(m_ref, t_ref, x_ref, s_ref, p_ref, d_ref, own_ref, *refs):
        pieces, outs = refs[:n_t], refs[n_t:-4]
        s_buf, p_buf, m_buf, sems = refs[-4:]
        row = pl.multiple_of((lax.axis_index("dp") % GROUP) * rows, rows)
        pairs = [
            (s_ref.at[:, :PB], s_buf),
            (p_ref.at[:, :PB], p_buf),
            (m_ref, m_buf),
            (x_ref, own_ref.at[:, :width]),
        ]
        for k in range(n_t):
            col = pl.multiple_of(((lax.axis_index("tensor") + k) % n_t) * width, width)
            pairs.append((d_ref.at[pl.ds(row, rows), pl.ds(col, width)], pieces[k]))
        if wide:
            for i in range(n_dp):
                pairs.append((t_ref.at[:, i * wide : (i + 1) * wide], outs[0].at[i, :tok]))
        copies = [
            pltpu.make_async_copy(src, dst, sems.at[i]) for i, (src, dst) in enumerate(pairs)
        ]
        for c in copies:
            c.start()
        for c in copies[:3]:
            c.wait()
        own_ref[:, width:] = scaled_difference(s_buf[...], p_buf[...], factor)
        line = lax.broadcasted_iota(jnp.int32, (16, tok), 0)
        number = jnp.broadcast_to(m_buf[...], (16, tok))
        high, low = number // LANES, number % LANES
        digits = jnp.where(line == 0, high, jnp.where(line == 1, low, 0))
        digits = digits.astype(jnp.float32).astype(jnp.bfloat16)
        if wide:
            for i in range(n_dp):
                outs[0][i, tok:, :] = jnp.zeros((16, wide), jnp.bfloat16)
                outs[0][i, tok:, :tok] = digits
        for c in copies[3:]:
            c.wait()

    shapes = [(tok, width + PB)] + [(rows, width)] * n_t
    if wide:
        shapes.append((n_dp, tok + 16, wide))
    out = pl.pallas_call(
        kernel,
        in_specs=[hbm] * 6,
        out_specs=[VMEM] * len(shapes),
        out_shape=[struct(s) for s in shapes],
        scratch_shapes=[
            pltpu.VMEM((tok, PB), jnp.bfloat16),
            pltpu.VMEM((tok, PB), jnp.bfloat16),
            pltpu.VMEM((1, tok), jnp.int32),
            pltpu.SemaphoreType.DMA((4 + n_t + n_dp,)),
        ],
        compiler_params=params(60),
        cost_estimate=cost(0, 1024),
        name="prepare",
    )(row_map.reshape(1, tok), teacher, mlp_input, student, projected, down)
    return out if wide else [*out, blocks]


def stack_rows(parts, rows, width, mib, after=()):
    def kernel(*refs):
        out_ref = refs[-1]
        for i, ref in enumerate(refs[: len(parts)]):
            out_ref[i * rows : (i + 1) * rows] = ref[ref.shape[0] - rows :, :width]

    return pl.pallas_call(
        kernel,
        in_specs=[VMEM] * len(parts) + [pl.BlockSpec(memory_space=pl.ANY)] * len(after),
        out_specs=VMEM,
        out_shape=struct((len(parts) * rows, width)),
        compiler_params=params(mib),
        cost_estimate=cost(0, 1024),
        name="stack_rows",
    )(*parts, *after)


def ordered(x, *after):
    def kernel(*refs):
        pass

    return pl.pallas_call(
        kernel,
        in_specs=[pl.BlockSpec(memory_space=pl.ANY)] * (1 + len(after)),
        out_specs=pl.BlockSpec(memory_space=pl.ANY),
        out_shape=struct(x.shape, x.dtype),
        input_output_aliases={0: 0},
        compiler_params=params(60),
        cost_estimate=cost(0, 1024),
        name="ordered",
    )(x, *after)


def partial_products(near, far, student, projected, n_t, rows, factor, after):
    tok, width = student.shape
    hb = rows * GROUP
    half = GROUP // 2

    def kernel(near_ref, far_ref, s_ref, p_ref, *refs):
        outs = refs[len(after) :]
        err = scaled_difference(s_ref[...], p_ref[...], factor)
        place = lax.axis_index("dp") % GROUP
        for side, ref in enumerate((near_ref, far_ref)):
            product = contract_cols(ref[...], err)
            for j in range(half):
                row = pl.multiple_of((place ^ (2 * j + side)) * rows, rows)
                for k in range(n_t):
                    at = (j * n_t + k) * rows
                    outs[k][pl.ds(row, rows), :] = product[at : at + rows]

    return pl.pallas_call(
        kernel,
        in_specs=[VMEM] * 4
        + [pl.BlockSpec(memory_space=pl.ANY)] * len(after),
        out_specs=[VMEM] * n_t,
        out_shape=[struct((hb, tok), jnp.float32)] * n_t,
        compiler_params=params(60),
        cost_estimate=cost(0, 1024),
        name="partial_products",
    )(near, far, student, projected, *after)


def weight_copies(gate_ref, up_ref, w_ref, sems, slots, width):
    hb = gate_ref.shape[1]
    copies = []
    for i, slot in enumerate(slots):
        at = pl.ds(pl.multiple_of(slot * width, width), width)
        for j, ref in enumerate((gate_ref, up_ref)):
            dst = w_ref.at[i, :, j * hb : (j + 1) * hb]
            copies.append(pltpu.make_async_copy(ref.at[at], dst, sems.at[2 * i + j]))
    return copies


def place_slices(slices, places, width, n_t, n_dp, after):
    count = slices[0].shape[0]
    cols = width * n_t // n_dp
    per = width // cols

    def kernel(*refs):
        out_ref = refs[-1]
        for k, x_ref in zip(places, refs):
            slot = (lax.axis_index("tensor") + n_t - k) % n_t
            for b in range(per):
                out_ref[slot * per + b] = x_ref[:, b * cols : (b + 1) * cols]

    return pl.pallas_call(
        kernel,
        in_specs=[VMEM] * len(slices) + [pl.BlockSpec(memory_space=pl.ANY)] * len(after),
        out_specs=VMEM,
        out_shape=struct((n_dp, count, cols)),
        compiler_params=params(60),
        cost_estimate=cost(0, 1024),
        name="place_slices",
    )(*slices, *after)


def place_last(payload, from_left, from_right, ends, width, n_t, after=()):
    n_dp = payload.shape[0]
    cols = width * n_t // n_dp
    per = width // cols
    aligned = cols % LANES == 0
    hbm = pl.BlockSpec(memory_space=pltpu.HBM)

    def kernel(in_ref, left_ref, right_ref, last_ref, first_ref, *refs):
        out_ref, sems = refs[len(after) :]
        t = lax.axis_index("tensor")
        if not aligned:
            out_ref[...] = in_ref[...]

        def place(ref, slot):
            if not aligned:
                for b in range(per):
                    out_ref[slot * per + b] = ref[:, b * cols : (b + 1) * cols]
                return
            copies = []
            for b in range(per):
                src = ref.at[:, pl.ds(b * cols, cols)]
                dst = out_ref.at[slot * per + b]
                copies.append(pltpu.make_async_copy(src, dst, sems.at[b]))
            for c in copies:
                c.start()

            for c in copies:
                c.wait()

        half = n_t // 2
        for ref, slot, here in (
            (left_ref, t - half, t >= half),
            (right_ref, t + half, t < half),
            (last_ref, 0, t == n_t - 1),
            (first_ref, n_t - 1, t == 0),
        ):
            pl.when(here)(functools.partial(place, ref, slot))

    return pl.pallas_call(
        kernel,
        in_specs=[hbm if aligned else VMEM]
        + [VMEM] * 4
        + [pl.BlockSpec(memory_space=pl.ANY)] * len(after),
        out_specs=hbm if aligned else VMEM,
        out_shape=struct(payload.shape),
        input_output_aliases={0: 0} if aligned else {},
        scratch_shapes=[pltpu.SemaphoreType.DMA((per,))],
        compiler_params=params(60),
        cost_estimate=cost(0, 1024),
        name="place_last",
    )(payload, from_left, from_right, *ends, *after)


def gate_and_up(slices, gate, up, n_t, after):
    count, width, hb = slices[0].shape[0], gate.shape[0] // n_t, gate.shape[1]
    n_s = len(slices)

    def kernel(*refs):
        xs, gate_ref, up_ref = refs[:n_s], refs[n_s], refs[n_s + 1]
        pre_ref, w_ref, sems = refs[-3:]
        t = lax.axis_index("tensor")
        slots = [t, (t + n_t - 1) % n_t, (t + 1) % n_t, (t + n_t // 2) % n_t]
        copies = weight_copies(gate_ref, up_ref, w_ref, sems, slots, width)
        for c in copies:
            c.start()
        left = jnp.where(t == 0, xs[6][:, :width], xs[1][:, :width])
        right = jnp.where(t == n_t - 1, xs[5][:, :width], xs[2][:, :width])
        away = jnp.where(t < n_t // 2, xs[4][:, :width], xs[3][:, :width])
        pre = jnp.zeros((count, 2 * hb), jnp.float32)
        for i, x in enumerate([xs[0][:, :width], left, right, away]):
            copies[2 * i].wait()
            copies[2 * i + 1].wait()
            pre += jnp.dot(x, w_ref[i], preferred_element_type=jnp.float32)
        pre_ref[...] = pre

    return pl.pallas_call(
        kernel,
        in_specs=[VMEM] * n_s
        + [pl.BlockSpec(memory_space=pltpu.HBM)] * 2
        + [pl.BlockSpec(memory_space=pl.ANY)] * len(after),
        out_specs=VMEM,
        out_shape=struct((count, 2 * hb), jnp.float32),
        scratch_shapes=[
            pltpu.VMEM((n_t, width, 2 * hb), jnp.bfloat16),
            pltpu.SemaphoreType.DMA((2 * n_t,)),
        ],
        compiler_params=params(60),
        cost_estimate=cost(0, 1024),
        name="gate_and_up",
    )(*slices, gate, up, *after)


def gradients(pre, acts, slices, width):
    count, hb = pre.shape[0], pre.shape[1] // 2

    def kernel(pre_ref, *refs):
        act_refs, xs, out_ref = refs[: len(acts)], refs[len(acts) : -1], refs[-1]
        act = act_refs[0][...]
        for ref in act_refs[1:]:
            act += ref[...]
        act = act.T
        gate_pre, up_pre = pre_ref[:, :hb], pre_ref[:, hb:]
        s = jax.nn.sigmoid(gate_pre)
        gate_grad = act * up_pre * s * (1.0 + gate_pre * (1.0 - s))
        up_grad = act * gate_pre * s
        out_ref[:, :hb] = gate_grad.astype(jnp.bfloat16)
        out_ref[:, hb : 2 * hb] = up_grad.astype(jnp.bfloat16)
        for i, ref in enumerate(xs):

            @pl.when(lax.axis_index("tensor") == i)
            def _(ref=ref):
                out_ref[:, 2 * hb :] = ref[...]

    bucket = pl.BlockSpec((count, PB), lambda i: (0, width // PB))

    def whole(x):
        return pl.BlockSpec(x.shape, lambda i: (0, 0))

    return pl.pallas_call(
        kernel,
        grid=(1,),
        in_specs=[whole(x) for x in (pre, *acts)] + [bucket] * len(slices),
        out_specs=pl.BlockSpec((count, 2 * hb + PB), lambda i: (0, 0)),
        out_shape=struct((count, 2 * hb + PB)),
        compiler_params=params(60),
        cost_estimate=cost(0, 1024),
        name="gradients",
    )(pre, *acts, *slices)


def hand_over(teach, tok):
    n_dp, _, wide = teach.shape
    groups = n_dp // GROUP
    span = GROUP * tok
    digits = []
    if wide < tok:
        digits = teach[:, tok:].reshape(n_dp, 2, tok)
        digits = [jnp.pad(digits, ((0, 0), (0, 14), (0, 0)))]

    def kernel(*refs):
        teach_ref, (out_ref, total_ref) = refs[0], refs[-2:]

        def receivers(h, carry):
            total_ref[...] = jnp.zeros_like(total_ref)

            def sender(g, carry):
                lines = refs[1][g] if digits else teach_ref[g, tok : tok + 16, :tok]
                lines = lines.astype(jnp.float32)
                number = (lines[0:1] * float(LANES) + lines[1:2]).astype(jnp.int32)
                token = lax.broadcasted_iota(jnp.int32, (span, tok), 0) + h * span
                picks = (token == number).astype(jnp.float32).astype(jnp.bfloat16)
                total_ref[...] += jnp.dot(
                    picks, teach_ref[g, :tok], preferred_element_type=jnp.float32
                )
                return carry

            lax.fori_loop(0, n_dp, sender, 0)
            out_ref[pl.ds(h * GROUP, GROUP)] = (
                total_ref[...].astype(jnp.bfloat16).reshape(GROUP, tok, wide)
            )
            return carry

        lax.fori_loop(0, groups, receivers, 0)

    return pl.pallas_call(
        kernel,
        in_specs=[VMEM] * (1 + len(digits)),
        out_specs=VMEM,
        out_shape=struct((n_dp, tok, wide)),
        scratch_shapes=[pltpu.VMEM((span, wide), jnp.float32)],
        compiler_params=params(60),
        cost_estimate=cost(0, 1024),
        name="hand_over",
    )(teach, *digits)


def final_product(feats, handed, grads, masks):
    n_dp, count, cols = feats.shape
    wide = handed.shape[2]
    hb = (grads[0].shape[-1] - PB) // 2

    def kernel(feats_ref, handed_ref, *refs):
        grad_refs, (proj_ref, gate_ref, up_ref) = refs[: len(grads)], refs[len(grads) : len(grads) + 3]

        def group(g, totals):
            here = pl.ds(g * GROUP, GROUP)
            left = left_ref[here].reshape(GROUP * count, 2 * hb + PB)
            right = feats_ref[here].reshape(GROUP * count, cols)
            rows = handed_ref[here].reshape(GROUP * count, wide)
            return (
                totals[0] + contract_rows(left[:, : 2 * hb], right),
                totals[1] + contract_rows(left[:, 2 * hb :], rows),
            )

        totals = (jnp.zeros((2 * hb, cols), jnp.float32), jnp.zeros((PB, wide), jnp.float32))
        if masks:
            left_ref = refs[-1]
            for mask, ref in zip(masks, grad_refs):
                left_ref[lax.axis_index("dp") ^ mask] = ref[:count]
                left_ref[lax.axis_index("dp") ^ mask ^ 1] = ref[count:]
            totals = group(0, totals)
        else:
            left_ref = grad_refs[0]
            totals = lax.fori_loop(0, n_dp // GROUP, group, totals)
        gate_ref[...] = totals[0][:hb]
        up_ref[...] = totals[0][hb:]
        proj_ref[...] = totals[1].reshape(PB, 1, wide)

    return pl.pallas_call(
        kernel,
        in_specs=[VMEM] * (2 + len(grads)),
        out_specs=[VMEM] * 3,
        out_shape=[struct((PB, 1, wide), jnp.float32)] + [struct((hb, cols), jnp.float32)] * 2,
        scratch_shapes=[pltpu.VMEM((n_dp, count, 2 * hb + PB), jnp.bfloat16)] if masks else [],
        compiler_params=params(40),
        cost_estimate=cost(0, 1024),
        name="final_product",
    )(feats, handed, *grads)


def body(
    teacher_rows, row_map, student_hidden, projected, mlp_input, gate_bucket, up_bucket, down_bucket
):
    tok = row_map.shape[0]
    n_dp = lax.axis_size("dp")
    n_t = lax.axis_size("tensor")
    hb, width = down_bucket.shape[0], student_hidden.shape[1]
    cols = width * n_t // n_dp
    factor = 1.0 / math.sqrt(tok * n_dp)
    rows = hb // GROUP

    own, *pieces, teach = prepare(
        row_map, teacher_rows, mlp_input, student_hidden, projected, down_bucket, n_dp, n_t, factor
    )
    rightward = [(i, i + 1) for i in range(n_t - 1)]
    leftward = [(i + 1, i) for i in range(n_t - 1)]
    teach = lax.all_to_all(teach, "dp", split_axis=0, concat_axis=0, tiled=True)
    mine = stack_rows(
        [pieces[0]] + [shift(pieces[k], n_t, k) for k in range(1, n_t)], rows, width, 8
    )
    others = [swap(mine, n_dp, mask) for mask in (2, 4, 6)]

    own = ordered(own, mine)
    from_left, from_right = hop(own, rightward), hop(own, leftward)
    far_left, far_right = hop(from_left, rightward[1:]), hop(from_right, leftward[:-1])
    ends = [hop(far_left, rightward[-1:]), hop(far_right, leftward[:1])]

    handed = hand_over(teach, tok)
    near = stack_rows([mine] + others, n_t * rows, width, 60)
    far = swap(near, n_dp, 1)
    partial = partial_products(near, far, student_hidden, projected, n_t, rows, factor, after=[])
    acts = [partial[0]] + [shift(partial[k], n_t, -k) for k in range(1, n_t)]

    sent = place_slices([own, from_left, from_right], [0, 1, n_t - 1], width, n_t, n_dp, [])
    sent = place_last(sent, far_left, far_right, ends, width, n_t, after=[partial[0], teach])
    feats = lax.all_to_all(sent, "dp", split_axis=0, concat_axis=0, tiled=True)

    slices = [own, from_left, from_right, far_left, far_right, *ends]
    pre = gate_and_up(slices, gate_bucket, up_bucket, n_t, after=[sent])
    grads = gradients(pre, acts, [own, from_left, far_left, ends[0]], width)
    masks = [0, 2, 4, 6] if n_dp == GROUP else []
    if masks:
        pair = stack_rows([grads, swap(grads, n_dp, 1)], tok, grads.shape[1], 8)
        grads = [pair] + [swap(pair, n_dp, mask) for mask in masks[1:]]
    else:
        grads = [lax.all_gather(grads, "dp")]
    return final_product(feats, handed, grads, masks)


def solution(mesh):
    in_specs = (
        P("dp", "tensor"),
        P("dp"),
        P("dp", "tensor"),
        P("dp", "tensor"),
        P("dp", "tensor"),
        P(None, "tensor"),
        P(None, "tensor"),
        P("tensor", None),
    )
    out_specs = (P(None, "tensor", "dp"), P("tensor", "dp"), P("tensor", "dp"))
    return jax.shard_map(body, mesh=mesh, in_specs=in_specs, out_specs=out_specs, check_vma=False)
```

```python
import functools
import math

import jax
import jax.numpy as jnp
from jax import lax
from jax.experimental import pallas as pl
from jax.experimental.pallas import tpu as pltpu
from jax.sharding import PartitionSpec as P

PB = 128
LANES = 128
GROUP = 8
MIB = 1 << 20

VMEM = pl.BlockSpec(memory_space=pltpu.VMEM)


def params(mib):
    return pltpu.CompilerParams(vmem_limit_bytes=mib * MIB)


def cost(flops, nbytes):
    return pl.CostEstimate(flops=int(flops), bytes_accessed=int(nbytes), transcendentals=0)


def struct(shape, dtype=jnp.bfloat16):
    return jax.ShapeDtypeStruct(shape, dtype)


def shift(x, count, by):
    return lax.ppermute(x, "tensor", [(i, (i + by) % count) for i in range(count)])


def hop(x, pairs):
    return lax.ppermute(x, "tensor", pairs)


def swap(x, count, mask):
    return lax.ppermute(x, "dp", [(i, i ^ mask) for i in range(count)])


def contract_rows(left, right):
    return lax.dot_general(
        left, right, (((0,), (0,)), ((), ())), preferred_element_type=jnp.float32
    )


def contract_cols(left, right):
    return lax.dot_general(
        left, right, (((1,), (1,)), ((), ())), preferred_element_type=jnp.float32
    )


def scaled_difference(student, projected, factor):
    wide = student.astype(jnp.float32) - projected.astype(jnp.float32)
    return (wide * factor).astype(jnp.bfloat16)


def prepare(row_map, teacher, mlp_input, student, projected, down, n_dp, n_t, factor):
    tok, width = mlp_input.shape
    rows = down.shape[0] // GROUP
    wide = teacher.shape[1] // n_dp
    hbm = pl.BlockSpec(memory_space=pltpu.HBM)
    if wide % LANES:
        blocks = teacher.reshape(tok, n_dp, wide).transpose(1, 0, 2)
        numbers = jnp.stack([row_map // LANES, row_map % LANES]).astype(jnp.bfloat16)
        numbers = jnp.broadcast_to(numbers.reshape(1, -1, wide), (n_dp, 2 * tok // wide, wide))
        blocks = jnp.concatenate([blocks, numbers], axis=1)
        wide = 0

    def kernel(m_ref, t_ref, x_ref, s_ref, p_ref, d_ref, own_ref, *refs):
        pieces, outs = refs[:n_t], refs[n_t:-4]
        s_buf, p_buf, m_buf, sems = refs[-4:]
        row = pl.multiple_of((lax.axis_index("dp") % GROUP) * rows, rows)
        pairs = [
            (s_ref.at[:, :PB], s_buf),
            (p_ref.at[:, :PB], p_buf),
            (m_ref, m_buf),
            (x_ref, own_ref.at[:, :width]),
        ]
        for k in range(n_t):
            col = pl.multiple_of(((lax.axis_index("tensor") + k) % n_t) * width, width)
            pairs.append((d_ref.at[pl.ds(row, rows), pl.ds(col, width)], pieces[k]))
        if wide:
            for i in range(n_dp):
                pairs.append((t_ref.at[:, i * wide : (i + 1) * wide], outs[0].at[i, :tok]))
        copies = [
            pltpu.make_async_copy(src, dst, sems.at[i]) for i, (src, dst) in enumerate(pairs)
        ]
        for c in copies:
            c.start()
        for c in copies[:3]:
            c.wait()
        own_ref[:, width:] = scaled_difference(s_buf[...], p_buf[...], factor)
        line = lax.broadcasted_iota(jnp.int32, (16, tok), 0)
        number = jnp.broadcast_to(m_buf[...], (16, tok))
        high, low = number // LANES, number % LANES
        digits = jnp.where(line == 0, high, jnp.where(line == 1, low, 0))
        digits = digits.astype(jnp.float32).astype(jnp.bfloat16)
        if wide:
            for i in range(n_dp):
                outs[0][i, tok:, :] = jnp.zeros((16, wide), jnp.bfloat16)
                outs[0][i, tok:, :tok] = digits
        for c in copies[3:]:
            c.wait()

    shapes = [(tok, width + PB)] + [(rows, width)] * n_t
    if wide:
        shapes.append((n_dp, tok + 16, wide))
    out = pl.pallas_call(
        kernel,
        in_specs=[hbm] * 6,
        out_specs=[VMEM] * len(shapes),
        out_shape=[struct(s) for s in shapes],
        scratch_shapes=[
            pltpu.VMEM((tok, PB), jnp.bfloat16),
            pltpu.VMEM((tok, PB), jnp.bfloat16),
            pltpu.VMEM((1, tok), jnp.int32),
            pltpu.SemaphoreType.DMA((4 + n_t + n_dp,)),
        ],
        compiler_params=params(60),
        cost_estimate=cost(0, 1024),
        name="prepare",
    )(row_map.reshape(1, tok), teacher, mlp_input, student, projected, down)
    return out if wide else [*out, blocks]


def stack_rows(parts, rows, width, mib, after=()):
    def kernel(*refs):
        out_ref = refs[-1]
        for i, ref in enumerate(refs[: len(parts)]):
            out_ref[i * rows : (i + 1) * rows] = ref[ref.shape[0] - rows :, :width]

    return pl.pallas_call(
        kernel,
        in_specs=[VMEM] * len(parts) + [pl.BlockSpec(memory_space=pl.ANY)] * len(after),
        out_specs=VMEM,
        out_shape=struct((len(parts) * rows, width)),
        compiler_params=params(mib),
        cost_estimate=cost(0, 1024),
        name="stack_rows",
    )(*parts, *after)


def ordered(x, *after):
    def kernel(*refs):
        pass

    return pl.pallas_call(
        kernel,
        in_specs=[pl.BlockSpec(memory_space=pl.ANY)] * (1 + len(after)),
        out_specs=pl.BlockSpec(memory_space=pl.ANY),
        out_shape=struct(x.shape, x.dtype),
        input_output_aliases={0: 0},
        compiler_params=params(60),
        cost_estimate=cost(0, 1024),
        name="ordered",
    )(x, *after)


def partial_products(near, far, student, projected, n_t, rows, factor, after):
    tok, width = student.shape
    hb = rows * GROUP
    half = GROUP // 2

    def kernel(near_ref, far_ref, s_ref, p_ref, *refs):
        outs = refs[len(after) :]
        err = scaled_difference(s_ref[...], p_ref[...], factor)
        place = lax.axis_index("dp") % GROUP
        for side, ref in enumerate((near_ref, far_ref)):
            product = contract_cols(ref[...], err)
            for j in range(half):
                row = pl.multiple_of((place ^ (2 * j + side)) * rows, rows)
                for k in range(n_t):
                    at = (j * n_t + k) * rows
                    outs[k][pl.ds(row, rows), :] = product[at : at + rows]

    return pl.pallas_call(
        kernel,
        in_specs=[VMEM] * 4
        + [pl.BlockSpec(memory_space=pl.ANY)] * len(after),
        out_specs=[VMEM] * n_t,
        out_shape=[struct((hb, tok), jnp.float32)] * n_t,
        compiler_params=params(60),
        cost_estimate=cost(0, 1024),
        name="partial_products",
    )(near, far, student, projected, *after)


def weight_copies(gate_ref, up_ref, w_ref, sems, slots, width):
    hb = gate_ref.shape[1]
    copies = []
    for i, slot in enumerate(slots):
        at = pl.ds(pl.multiple_of(slot * width, width), width)
        for j, ref in enumerate((gate_ref, up_ref)):
            dst = w_ref.at[i, :, j * hb : (j + 1) * hb]
            copies.append(pltpu.make_async_copy(ref.at[at], dst, sems.at[2 * i + j]))
    return copies


def place_slices(slices, places, width, n_t, n_dp, after):
    count = slices[0].shape[0]
    cols = width * n_t // n_dp
    per = width // cols

    def kernel(*refs):
        out_ref = refs[-1]
        for k, x_ref in zip(places, refs):
            slot = (lax.axis_index("tensor") + n_t - k) % n_t
            for b in range(per):
                out_ref[slot * per + b] = x_ref[:, b * cols : (b + 1) * cols]

    return pl.pallas_call(
        kernel,
        in_specs=[VMEM] * len(slices) + [pl.BlockSpec(memory_space=pl.ANY)] * len(after),
        out_specs=VMEM,
        out_shape=struct((n_dp, count, cols)),
        compiler_params=params(60),
        cost_estimate=cost(0, 1024),
        name="place_slices",
    )(*slices, *after)


def place_last(payload, from_left, from_right, ends, width, n_t, after=()):
    n_dp = payload.shape[0]
    cols = width * n_t // n_dp
    per = width // cols
    aligned = cols % LANES == 0
    hbm = pl.BlockSpec(memory_space=pltpu.HBM)

    def kernel(in_ref, left_ref, right_ref, last_ref, first_ref, *refs):
        out_ref, sems = refs[len(after) :]
        t = lax.axis_index("tensor")
        if not aligned:
            out_ref[...] = in_ref[...]

        def place(ref, slot):
            if not aligned:
                for b in range(per):
                    out_ref[slot * per + b] = ref[:, b * cols : (b + 1) * cols]
                return
            copies = []
            for b in range(per):
                src = ref.at[:, pl.ds(b * cols, cols)]
                dst = out_ref.at[slot * per + b]
                copies.append(pltpu.make_async_copy(src, dst, sems.at[b]))
            for c in copies:
                c.start()

            for c in copies:
                c.wait()

        half = n_t // 2
        for ref, slot, here in (
            (left_ref, t - half, t >= half),
            (right_ref, t + half, t < half),
            (last_ref, 0, t == n_t - 1),
            (first_ref, n_t - 1, t == 0),
        ):
            pl.when(here)(functools.partial(place, ref, slot))

    return pl.pallas_call(
        kernel,
        in_specs=[hbm if aligned else VMEM]
        + [VMEM] * 4
        + [pl.BlockSpec(memory_space=pl.ANY)] * len(after),
        out_specs=hbm if aligned else VMEM,
        out_shape=struct(payload.shape),
        input_output_aliases={0: 0} if aligned else {},
        scratch_shapes=[pltpu.SemaphoreType.DMA((per,))],
        compiler_params=params(12 if aligned else 60),
        cost_estimate=cost(0, 1024),
        name="place_last",
    )(payload, from_left, from_right, *ends, *after)


def gate_and_up(slices, gate, up, n_t, after):
    count, width, hb = slices[0].shape[0], gate.shape[0] // n_t, gate.shape[1]
    n_s = len(slices)

    def kernel(*refs):
        xs, gate_ref, up_ref = refs[:n_s], refs[n_s], refs[n_s + 1]
        pre_ref, w_ref, sems = refs[-3:]
        t = lax.axis_index("tensor")
        slots = [t, (t + n_t - 1) % n_t, (t + 1) % n_t, (t + n_t // 2) % n_t]
        copies = weight_copies(gate_ref, up_ref, w_ref, sems, slots, width)
        for c in copies:
            c.start()
        left = jnp.where(t == 0, xs[6][:, :width], xs[1][:, :width])
        right = jnp.where(t == n_t - 1, xs[5][:, :width], xs[2][:, :width])
        away = jnp.where(t < n_t // 2, xs[4][:, :width], xs[3][:, :width])
        pre = jnp.zeros((count, 2 * hb), jnp.float32)
        for i, x in enumerate([xs[0][:, :width], left, right, away]):
            copies[2 * i].wait()
            copies[2 * i + 1].wait()
            pre += jnp.dot(x, w_ref[i], preferred_element_type=jnp.float32)
        pre_ref[...] = pre

    return pl.pallas_call(
        kernel,
        in_specs=[VMEM] * n_s
        + [pl.BlockSpec(memory_space=pltpu.HBM)] * 2
        + [pl.BlockSpec(memory_space=pl.ANY)] * len(after),
        out_specs=VMEM,
        out_shape=struct((count, 2 * hb), jnp.float32),
        scratch_shapes=[
            pltpu.VMEM((n_t, width, 2 * hb), jnp.bfloat16),
            pltpu.SemaphoreType.DMA((2 * n_t,)),
        ],
        compiler_params=params(60),
        cost_estimate=cost(0, 1024),
        name="gate_and_up",
    )(*slices, gate, up, *after)


def gradients(pre, acts, slices, width):
    count, hb = pre.shape[0], pre.shape[1] // 2

    def kernel(pre_ref, *refs):
        act_refs, xs, out_ref = refs[: len(acts)], refs[len(acts) : -1], refs[-1]
        act = act_refs[0][...]
        for ref in act_refs[1:]:
            act += ref[...]
        act = act.T
        gate_pre, up_pre = pre_ref[:, :hb], pre_ref[:, hb:]
        s = jax.nn.sigmoid(gate_pre)
        gate_grad = act * up_pre * s * (1.0 + gate_pre * (1.0 - s))
        up_grad = act * gate_pre * s
        out_ref[:, :hb] = gate_grad.astype(jnp.bfloat16)
        out_ref[:, hb : 2 * hb] = up_grad.astype(jnp.bfloat16)
        for i, ref in enumerate(xs):

            @pl.when(lax.axis_index("tensor") == i)
            def _(ref=ref):
                out_ref[:, 2 * hb :] = ref[...]

    bucket = pl.BlockSpec((count, PB), lambda i: (0, width // PB))

    def whole(x):
        return pl.BlockSpec(x.shape, lambda i: (0, 0))

    return pl.pallas_call(
        kernel,
        grid=(1,),
        in_specs=[whole(x) for x in (pre, *acts)] + [bucket] * len(slices),
        out_specs=pl.BlockSpec((count, 2 * hb + PB), lambda i: (0, 0)),
        out_shape=struct((count, 2 * hb + PB)),
        compiler_params=params(60),
        cost_estimate=cost(0, 1024),
        name="gradients",
    )(pre, *acts, *slices)


def hand_over(teach, tok):
    n_dp, _, wide = teach.shape
    groups = n_dp // GROUP
    span = GROUP * tok
    digits = []
    if wide < tok:
        digits = teach[:, tok:].reshape(n_dp, 2, tok)
        digits = [jnp.pad(digits, ((0, 0), (0, 14), (0, 0)))]

    def kernel(*refs):
        teach_ref, (out_ref, total_ref) = refs[0], refs[-2:]

        def receivers(h, carry):
            total_ref[...] = jnp.zeros_like(total_ref)

            def sender(g, carry):
                lines = refs[1][g] if digits else teach_ref[g, tok : tok + 16, :tok]
                lines = lines.astype(jnp.float32)
                number = (lines[0:1] * float(LANES) + lines[1:2]).astype(jnp.int32)
                token = lax.broadcasted_iota(jnp.int32, (span, tok), 0) + h * span
                picks = (token == number).astype(jnp.float32).astype(jnp.bfloat16)
                total_ref[...] += jnp.dot(
                    picks, teach_ref[g, :tok], preferred_element_type=jnp.float32
                )
                return carry

            lax.fori_loop(0, n_dp, sender, 0)
            out_ref[pl.ds(h * GROUP, GROUP)] = (
                total_ref[...].astype(jnp.bfloat16).reshape(GROUP, tok, wide)
            )
            return carry

        lax.fori_loop(0, groups, receivers, 0)

    return pl.pallas_call(
        kernel,
        in_specs=[VMEM] * (1 + len(digits)),
        out_specs=VMEM,
        out_shape=struct((n_dp, tok, wide)),
        scratch_shapes=[pltpu.VMEM((span, wide), jnp.float32)],
        compiler_params=params(60),
        cost_estimate=cost(0, 1024),
        name="hand_over",
    )(teach, *digits)


def final_product(feats, handed, grads, masks):
    n_dp, count, cols = feats.shape
    wide = handed.shape[2]
    hb = (grads[0].shape[-1] - PB) // 2

    def kernel(feats_ref, handed_ref, *refs):
        grad_refs, (proj_ref, gate_ref, up_ref) = refs[: len(grads)], refs[len(grads) : len(grads) + 3]

        def group(g, totals):
            here = pl.ds(g * GROUP, GROUP)
            left = left_ref[here].reshape(GROUP * count, 2 * hb + PB)
            right = feats_ref[here].reshape(GROUP * count, cols)
            rows = handed_ref[here].reshape(GROUP * count, wide)
            return (
                totals[0] + contract_rows(left[:, : 2 * hb], right),
                totals[1] + contract_rows(left[:, 2 * hb :], rows),
            )

        totals = (jnp.zeros((2 * hb, cols), jnp.float32), jnp.zeros((PB, wide), jnp.float32))
        if masks:
            left_ref = refs[-1]
            for mask, ref in zip(masks, grad_refs):
                left_ref[lax.axis_index("dp") ^ mask] = ref[:count]
                left_ref[lax.axis_index("dp") ^ mask ^ 1] = ref[count:]
            totals = group(0, totals)
        else:
            left_ref = grad_refs[0]
            totals = lax.fori_loop(0, n_dp // GROUP, group, totals)
        gate_ref[...] = totals[0][:hb]
        up_ref[...] = totals[0][hb:]
        proj_ref[...] = totals[1].reshape(PB, 1, wide)

    return pl.pallas_call(
        kernel,
        in_specs=[VMEM] * (2 + len(grads)),
        out_specs=[VMEM] * 3,
        out_shape=[struct((PB, 1, wide), jnp.float32)] + [struct((hb, cols), jnp.float32)] * 2,
        scratch_shapes=[pltpu.VMEM((n_dp, count, 2 * hb + PB), jnp.bfloat16)] if masks else [],
        compiler_params=params(40),
        cost_estimate=cost(0, 1024),
        name="final_product",
    )(feats, handed, *grads)


def body(
    teacher_rows, row_map, student_hidden, projected, mlp_input, gate_bucket, up_bucket, down_bucket
):
    tok = row_map.shape[0]
    n_dp = lax.axis_size("dp")
    n_t = lax.axis_size("tensor")
    hb, width = down_bucket.shape[0], student_hidden.shape[1]
    cols = width * n_t // n_dp
    factor = 1.0 / math.sqrt(tok * n_dp)
    rows = hb // GROUP

    own, *pieces, teach = prepare(
        row_map, teacher_rows, mlp_input, student_hidden, projected, down_bucket, n_dp, n_t, factor
    )
    rightward = [(i, i + 1) for i in range(n_t - 1)]
    leftward = [(i + 1, i) for i in range(n_t - 1)]
    teach = lax.all_to_all(teach, "dp", split_axis=0, concat_axis=0, tiled=True)
    mine = stack_rows(
        [pieces[0]] + [shift(pieces[k], n_t, k) for k in range(1, n_t)], rows, width, 8
    )
    others = [swap(mine, n_dp, mask) for mask in (2, 4, 6)]

    own = ordered(own, mine)
    from_left, from_right = hop(own, rightward), hop(own, leftward)
    far_left, far_right = hop(from_left, rightward[1:]), hop(from_right, leftward[:-1])
    ends = [hop(far_left, rightward[-1:]), hop(far_right, leftward[:1])]

    handed = hand_over(teach, tok)
    near = stack_rows([mine] + others, n_t * rows, width, 60)
    far = swap(near, n_dp, 1)
    partial = partial_products(near, far, student_hidden, projected, n_t, rows, factor, after=[])
    acts = [partial[0]] + [shift(partial[k], n_t, -k) for k in range(1, n_t)]

    sent = place_slices([own, from_left, from_right], [0, 1, n_t - 1], width, n_t, n_dp, [])
    sent = place_last(sent, far_left, far_right, ends, width, n_t, after=[partial[0], teach])
    feats = lax.all_to_all(sent, "dp", split_axis=0, concat_axis=0, tiled=True)

    slices = [own, from_left, from_right, far_left, far_right, *ends]
    pre = gate_and_up(slices, gate_bucket, up_bucket, n_t, after=[sent])
    grads = gradients(pre, acts, [own, from_left, far_left, ends[0]], width)
    masks = [0, 2, 4, 6] if n_dp == GROUP else []
    if masks:
        pair = stack_rows([grads, swap(grads, n_dp, 1)], tok, grads.shape[1], 8)
        grads = [pair] + [swap(pair, n_dp, mask) for mask in masks[1:]]
    else:
        grads = [lax.all_gather(grads, "dp")]
    return final_product(feats, handed, grads, masks)


def solution(mesh):
    in_specs = (
        P("dp", "tensor"),
        P("dp"),
        P("dp", "tensor"),
        P("dp", "tensor"),
        P("dp", "tensor"),
        P(None, "tensor"),
        P(None, "tensor"),
        P("tensor", None),
    )
    out_specs = (P(None, "tensor", "dp"), P("tensor", "dp"), P("tensor", "dp"))
    return jax.shard_map(body, mesh=mesh, in_specs=in_specs, out_specs=out_specs, check_vma=False)
```
